256 devices in a mesh: gz: 8 (over z_lo, core), gy: 32 (over z_hi, x, y).
Axes of the slice: x: 4, y: 4, z: 8 (z_hi: 2, z_lo: 4; z = z_hi * 4 + z_lo), core: 2. Of those that a mesh axis runs over, the one named last changes fastest.
Arguments:
- features: bfloat16 [64, 16, 64, 128], P(None, 'gz', 'gy'), may hold values from -6 to 6
- up_weight: bfloat16 [64, 32, 4, 4, 4], replicated, may hold values from -0.25 to 0.25
- conv_weight: bfloat16 [32, 32, 3, 3, 3], replicated, may hold values from -0.21875 to 0.21875
- out_grad: bfloat16 [32, 32, 128, 256], P(None, 'gz', 'gy'), may hold values from -6 to 6
- labels: int32 [32, 128, 256], P('gz', 'gy'), may hold values 0 or 1
Outputs:
- decoded: bfloat16 [32, 32, 128, 256], P(None, 'gz', 'gy')
- features_grad: bfloat16 [64, 16, 64, 128], P(None, 'gz', 'gy')
- up_weight_grad: float32 [64, 32, 4, 4, 4], replicated
- conv_weight_grad: float32 [32, 32, 3, 3, 3], replicated
The draws below stay inside these ranges and needn't reach their ends.
Inputs may be any that keep to these rules, and one draw needn't show every extreme that they name: `labels`: 1 marks an annotated voxel, 0 an unannotated one.
All inputs are finite; a program needn't handle non-finite values. No bound on the sum of `labels` on one device may be relied on, other than what follows from the above.
Results may differ from the reference program's by a relative error of at most 0.02.
Values may be sent and summed in bfloat16 or wider, within the bound.
A program may use at most 64 MiB of HBM per device.

```python
import math
import jax
import jax.numpy as jnp
from jax import lax

CIN = 64
CMID = 32
COUT = 32
XO = 256
ZOUT = 32
YOUT = 128
ZIN = 16
YIN = 64
XIN = 128


def plant(drawn, stream_key, smallest, high):
    shape = drawn.shape
    place = [jax.random.randint(jax.random.fold_in(stream_key, axis), (), 0, shape[axis]) for axis in range(len(shape))]
    drawn = drawn.at[tuple(place)].set(smallest)
    longest = shape.index(max(shape))
    place[longest] = (place[longest] + 1) % shape[longest]
    return drawn.at[tuple(place)].set(high)


def block_scale(own_key, shape, shards, least, top_value):
    loudness = 1.0
    for axis_at, shards_of in shards:
        heights = jax.random.uniform(jax.random.fold_in(jax.random.fold_in(own_key, 6), axis_at), (shards_of,), jnp.float32, least / len(shards), top_value / len(shards))
        loudness = loudness * jnp.repeat(jnp.exp(heights), shape[axis_at] // shards_of).reshape((-1,) + (1,) * (len(shape) - 1 - axis_at))
    return loudness


def noise(stream_key, shape, width, bound, cuts=(), dtype=jnp.bfloat16):
    loudness = block_scale(stream_key, shape, cuts, -0.22, 0.18) if cuts else 1.0
    array = jax.random.normal(stream_key, shape, jnp.float32) * width * loudness
    return jnp.minimum(jnp.maximum(array, -bound), bound).astype(dtype)


def setup_inputs(seed: int = 0) -> dict:
    keys = jax.random.split(jax.random.key(seed), 6)
    return {
        "features": noise(keys[0], (CIN, ZIN, YIN, XIN), 1.0, 6.0, ((1, 8), (2, 32))),
        "up_weight": noise(keys[1], (CIN, CMID, 4, 4, 4), (8 * CIN) ** -0.5, 0.25),
        "conv_weight": noise(keys[2], (COUT, CMID, 3, 3, 3), (27 * CMID) ** -0.5, 0.21875),
        "out_grad": noise(keys[3], (COUT, ZOUT, YOUT, XO), 1.0, 6.0, ((1, 8), (2, 32))),
        "labels": plant((jax.random.randint(keys[4], (ZOUT, YOUT, XO), 0, 3) < 2).astype(jnp.int32), jax.random.fold_in(keys[4], 1), 0, 1),
    }


def widen(block):
    return jnp.pad(block, ((0, 0), (1, 1), (1, 1), (1, 1)))

def window(padded, anchor, extent):
    limit = tuple((a + b for a, b in zip(anchor, extent)))
    return lax.slice(padded, (0,) + tuple(anchor), (padded.shape[0],) + limit)

def upsample_exact(features, up_weight):
    channels_in, extent_z, extent_y, extent_x = features.shape
    channels = up_weight.shape[1]
    padded = widen(features.astype(jnp.float32))
    weights = up_weight.astype(jnp.float32)
    results = []
    for parity_z in range(2):
        for parity_y in range(2):
            for parity_x in range(2):
                summed = jnp.zeros((channels, extent_z, extent_y, extent_x), jnp.float32)
                for offset_z in range(2):
                    for offset_y in range(2):
                        for offset_x in range(2):
                            piece = window(padded, (parity_z + offset_z, parity_y + offset_y, parity_x + offset_x), (extent_z, extent_y, extent_x))
                            matrix = weights[:, :, 3 - 2 * offset_z - parity_z, 3 - 2 * offset_y - parity_y, 3 - 2 * offset_x - parity_x]
                            summed = summed + jnp.einsum('ic,izyx->czyx', matrix, piece, precision=lax.Precision.HIGHEST)
                results.append(summed)
    joined = jnp.stack(results, axis=0).reshape(2, 2, 2, channels, extent_z, extent_y, extent_x)
    joined = jnp.transpose(joined, (3, 4, 0, 5, 1, 6, 2))
    return joined.reshape(channels, 2 * extent_z, 2 * extent_y, 2 * extent_x)

def stencil_exact(padded, weight):
    extent = (padded.shape[1] - 2, padded.shape[2] - 2, padded.shape[3] - 2)
    summed = jnp.zeros((weight.shape[0],) + extent, jnp.float32)
    for kernel_z in range(3):
        for kernel_y in range(3):
            for kernel_x in range(3):
                piece = window(padded, (kernel_z, kernel_y, kernel_x), extent)
                summed = summed + jnp.einsum('oc,czyx->ozyx', weight[:, :, kernel_z, kernel_y, kernel_x], piece, precision=lax.Precision.HIGHEST)
    return summed

def stencil_grad_exact(padded, cotangent):
    extent = cotangent.shape[1:]
    results = []
    for kernel_z in range(3):
        for kernel_y in range(3):
            for kernel_x in range(3):
                piece = window(padded, (kernel_z, kernel_y, kernel_x), extent)
                results.append(jnp.einsum('ozyx,czyx->oc', cotangent, piece, precision=lax.Precision.HIGHEST))
    joined = jnp.stack(results, axis=0).reshape((3, 3, 3) + results[0].shape)
    return jnp.transpose(joined, (3, 4, 0, 1, 2))

def coarse_exact(features, padded_grad, up_weight):
    channels_in, extent_z, extent_y, extent_x = features.shape
    channels = padded_grad.shape[0]
    feature_grad = jnp.zeros(features.shape, jnp.float32)
    results = []
    for kernel_z in range(4):
        for kernel_y in range(4):
            for kernel_x in range(4):
                piece = lax.slice(padded_grad, (0, kernel_z, kernel_y, kernel_x), (channels, kernel_z + 2 * extent_z - 1, kernel_y + 2 * extent_y - 1, kernel_x + 2 * extent_x - 1), (1, 2, 2, 2))
                matrix = up_weight[:, :, kernel_z, kernel_y, kernel_x]
                feature_grad = feature_grad + jnp.einsum('ic,czyx->izyx', matrix, piece, precision=lax.Precision.HIGHEST)
                results.append(jnp.einsum('izyx,czyx->ic', features, piece, precision=lax.Precision.HIGHEST))
    joined = jnp.stack(results, axis=0).reshape(4, 4, 4, channels_in, channels)
    return (feature_grad, jnp.transpose(joined, (3, 4, 0, 1, 2)))

def reference(features, up_weight, conv_weight, out_grad, labels):
    lifted = upsample_exact(features, up_weight)
    hidden = jnp.maximum(lifted, 0.0).astype(jnp.bfloat16)
    hidden_padded = widen(hidden.astype(jnp.float32))
    conv_exact = conv_weight.astype(jnp.float32)
    decoded = stencil_exact(hidden_padded, conv_exact).astype(jnp.bfloat16)
    cotangent = (out_grad * labels.astype(jnp.bfloat16)[None]).astype(jnp.float32)
    back_weight = jnp.transpose(jnp.flip(conv_exact, (2, 3, 4)), (1, 0, 2, 3, 4))
    before = stencil_exact(widen(cotangent), back_weight)
    hidden_grad = jnp.where(hidden > 0, before, 0.0).astype(jnp.bfloat16)
    conv_terms = stencil_grad_exact(hidden_padded, cotangent)
    features_grad, up_terms = coarse_exact(features.astype(jnp.float32), widen(hidden_grad.astype(jnp.float32)), up_weight.astype(jnp.float32))
    up_grad = up_terms * (1.0 / math.sqrt(ZIN * YIN * XIN))
    conv_grad = conv_terms * (1.0 / math.sqrt(ZOUT * YOUT * XO))
    return (decoded, features_grad.astype(jnp.bfloat16), up_grad, conv_grad)
```

```python
import math

import jax
import jax.numpy as jnp
from jax import lax
from jax.experimental import pallas as pl
from jax.experimental.pallas import tpu as pltpu
from jax.sharding import PartitionSpec as P

BF = jnp.bfloat16
F32 = jnp.float32
MESH = pl.DeviceIdType.MESH

NZ, NY = 8, 32
DIRECTIONS = [(dz, dy) for dz in (-1, 0, 1) for dy in (-1, 0, 1) if (dz, dy) != (0, 0)]
PIECE = 48
HALF = 16 * PIECE


def mm(a, b):
    return lax.dot_general(a, b, (((1,), (0,)), ((), ())), preferred_element_type=F32)


def mm_nt(a, b):
    return lax.dot_general(a, b, (((1,), (1,)), ((), ())), preferred_element_type=F32)


def mm_tn(a, b):
    return lax.dot_general(a, b, (((0,), (0,)), ((), ())), preferred_element_type=F32)


def one_hot(rows, cols, place):
    row = lax.broadcasted_iota(jnp.int32, (rows, cols), 0)
    col = lax.broadcasted_iota(jnp.int32, (rows, cols), 1)
    return jnp.where(place(row) == col, 1.0, 0.0).astype(BF)


def lane_masks(rows):
    lane = lax.broadcasted_iota(jnp.int32, (rows, 128), 1)
    return lane == 0, lane == 127


def before_lane(x, first):
    return jnp.where(first, 0.0, pltpu.roll(x, 1, 1))


def after_lane(x, last):
    return jnp.where(last, 0.0, pltpu.roll(x, 127, 1))


def halo_source(step, extent):
    if step == 0:
        return pl.ds(1, extent)
    return pl.ds(extent, 1) if step == 1 else pl.ds(1, 1)


def halo_target(step, extent):
    if step == 0:
        return pl.ds(1, extent)
    return pl.ds(0, 1) if step == 1 else pl.ds(extent + 1, 1)


def kernel(
    feat_ref, up_ref, conv_ref, og_ref, lab_ref,
    dec_ref, fgrad_ref, ugrad_ref, cgrad_ref,
    fh, ch, gh, fx, hx, cx, hgx, he,
    upf, uwt, t_up, t_fwd, t_bwd, dec,
    part, got0, pair, got1, got2, full,
    f_send, f_recv, c_send, c_recv, g_send, g_recv,
    s0_send, s0_recv, s1_send, s1_recv, s2_send, s2_recv, s3_send, s3_recv, s4_send, s4_recv,
):
    gz = lax.axis_index("gz")
    gy = lax.axis_index("gy")
    core = gz % 2
    z_lo = gz // 2
    z_hi = gy // 16
    xy = gy % 16
    chip_z = z_hi * 4 + z_lo
    partner = (gz + 1 - 2 * core, gy)

    def xy_peer(step):
        q = (xy + step) % 16
        return q, (gz, z_hi * 16 + q)

    def z_peer(step):
        q = (chip_z + step) % 8
        return q, ((q % 4) * 2 + core, (q // 4) * 16 + xy)

    def exists(dz, dy):
        return (gz + dz >= 0) & (gz + dz < NZ) & (gy + dy >= 0) & (gy + dy < NY)

    for buf, n in ((fh, 2), (ch, 4), (gh, 4)):
        for line in (0, n + 1):
            buf[line] = jnp.zeros(buf.shape[1:], BF)
            for k in range(1, n + 1):
                buf[k, line] = jnp.zeros(buf.shape[2:], BF)

    barrier = pltpu.get_barrier_semaphore()
    for dz, dy in DIRECTIONS:
        @pl.when(exists(dz, dy))
        def _():
            pl.semaphore_signal(barrier, 1, device_id=(gz + dz, gy + dy), device_id_type=MESH)
    pl.semaphore_signal(barrier, 1, device_id=partner, device_id_type=MESH)

    @pl.loop(1, 16)
    def _(step):
        pl.semaphore_signal(barrier, 1, device_id=xy_peer(step)[1], device_id_type=MESH)

    @pl.loop(1, 8)
    def _(step):
        pl.semaphore_signal(barrier, 1, device_id=z_peer(step)[1], device_id_type=MESH)

    local = mm(one_hot(256, 256, lambda r: (r & 63) * 4 + (r >> 6)), feat_ref[...]).astype(BF)
    for k in range(4):
        fh[1 + k // 2, 1 + k % 2] = local[k * 64 : (k + 1) * 64]
    split = one_hot(256, 256, lambda r: (r & 1) * 128 + (r >> 1))
    masked = (og_ref[...].reshape(32, 16, 256) * lab_ref[...].astype(BF)[None]).reshape(512, 256)
    rows = mm(one_hot(512, 512, lambda r: (r & 31) * 16 + (r >> 5)), masked).astype(BF)
    local = mm(rows, split).astype(BF)
    for k in range(16):
        ch[1 + k // 4, 1 + k % 4] = local[k * 32 : (k + 1) * 32]

    beside = 1 * (gz > 0) + 1 + 1 * (gz < NZ - 1)
    beside = beside * (1 * (gy > 0) + 1 + 1 * (gy < NY - 1)) - 1
    pl.semaphore_wait(barrier, beside + 1 + 15 + 7)

    def halo_copy(buf, extent, index, send, recv):
        dz, dy = DIRECTIONS[index]
        return pltpu.make_async_remote_copy(
            src_ref=buf.at[halo_source(dz, extent), halo_source(dy, extent)],
            dst_ref=buf.at[halo_target(dz, extent), halo_target(dy, extent)],
            send_sem=send.at[index],
            recv_sem=recv.at[index],
            device_id=(gz + dz, gy + dy),
            device_id_type=MESH,
        )

    def halo_start(*what):
        for index, (dz, dy) in enumerate(DIRECTIONS):
            @pl.when(exists(dz, dy))
            def _():
                halo_copy(what[0], what[1], index, what[2], what[3]).start()

    def halo_arrived(*what):
        for index, (dz, dy) in enumerate(DIRECTIONS):
            @pl.when(exists(-dz, -dy))
            def _():
                halo_copy(what[0], what[1], index, what[2], what[3]).wait_recv()

    def halo_sent(*what):
        for index, (dz, dy) in enumerate(DIRECTIONS):
            @pl.when(exists(dz, dy))
            def _():
                halo_copy(what[0], what[1], index, what[2], what[3]).wait_send()

    f_halo = (fh, 2, f_send, f_recv)
    c_halo = (ch, 4, c_send, c_recv)
    g_halo = (gh, 4, g_send, g_recv)
    halo_start(*f_halo)
    halo_start(*c_halo)

    upf[...] = up_ref[...].astype(F32)

    @pl.loop(0, 64)
    def _(k):
        uwt[k] = upf[pl.ds(k, 32, stride=64), :].astype(BF)

    for sz in range(2):
        for sy in range(2):
            for px in range(2):
                blocks = []
                for uz in range(2):
                    for uy in range(2):
                        base = (2 * (1 - uz) + sz) * 16 + (2 * (1 - uy) + sy) * 4
                        none = jnp.zeros((32, 64), BF)
                        if px == 0:
                            blocks += [uwt[base + 3], uwt[base + 1], none]
                        else:
                            blocks += [none, uwt[base + 2], uwt[base]]
                at = ((sz * 2 + sy) * 2 + px) * 32
                t_up[at : at + 32, :] = jnp.concatenate(blocks, axis=1)
    zero = jnp.zeros((32, 96), BF)
    taps = {}
    back = {}
    for dz in range(3):
        for dy in range(3):
            at = (dz * 3 + dy) * 96
            taps[dz, dy] = jnp.concatenate(
                [conv_ref[at + 32 * dx : at + 32 * dx + 32, :] for dx in range(3)], axis=1
            )
            back[2 - dz, 2 - dy] = conv_ref[at : at + 96, :].T
    for yo in range(4):
        for matrix, source in ((t_fwd, taps), (t_bwd, back)):
            matrix[yo * 32 : yo * 32 + 32, :] = jnp.concatenate(
                [
                    source[dz, yi - yo] if 0 <= yi - yo < 3 else zero
                    for dz in range(3)
                    for yi in range(6)
                ],
                axis=1,
            )

    halo_arrived(*f_halo)
    first64, last64 = lane_masks(64)
    first, last = lane_masks(32)
    for k in range(16):
        row = fh[k // 4, k % 4]
        wide = row.astype(F32)
        fx[k, 0:64] = before_lane(wide, first64).astype(BF)
        fx[k, 64:128] = row
        fx[k, 128:192] = after_lane(wide, last64).astype(BF)

    @pl.loop(0, 3)
    def _(jz):
        columns = []
        for jy in range(3):
            columns.append(
                jnp.concatenate(
                    [fx[(jz + uz) * 4 + jy + uy] for uz in range(2) for uy in range(2)], axis=0
                )
            )
        lifted = jnp.maximum(mm(t_up[...], jnp.concatenate(columns, axis=1)), 0.0)
        for sz in range(2):
            for sy in range(2):
                for jy in range(3):
                    at = (sz * 2 + sy) * 64
                    even = lifted[at : at + 32, jy * 128 : jy * 128 + 128]
                    odd = lifted[at + 32 : at + 64, jy * 128 : jy * 128 + 128]
                    zo, yo = jz * 2 + sz, jy * 2 + sy
                    at = pl.multiple_of((zo * 6 + yo) * 96, 32)
                    even_b, odd_b = even.astype(BF), odd.astype(BF)
                    hx[pl.ds(at, 32), 0:128] = before_lane(odd, first).astype(BF)
                    hx[pl.ds(at, 32), 128:256] = even_b
                    hx[pl.ds(at + 32, 32), 0:128] = even_b
                    hx[pl.ds(at + 32, 32), 128:256] = odd_b
                    hx[pl.ds(at + 64, 32), 0:128] = odd_b
                    hx[pl.ds(at + 64, 32), 128:256] = after_lane(even, last).astype(BF)
                    he[zo, yo, :, 0:128] = even_b
                    he[zo, yo, :, 128:256] = odd_b

    @pl.when(gz == 0)
    def _():
        hx[0:576] = jnp.zeros((576, 256), BF)

    @pl.when(gz == NZ - 1)
    def _():
        hx[2880:3456] = jnp.zeros((576, 256), BF)

    @pl.when(gy == 0)
    def _():
        for zi in range(6):
            hx[zi * 576 : zi * 576 + 96] = jnp.zeros((96, 256), BF)

    @pl.when(gy == NY - 1)
    def _():
        for zi in range(6):
            hx[zi * 576 + 480 : zi * 576 + 576] = jnp.zeros((96, 256), BF)

    halo_arrived(*c_halo)

    @pl.loop(0, 6)
    def _(zi):
        for yi in range(6):
            row = ch[zi, yi]
            even_b, odd_b = row[:, 0:128], row[:, 128:256]
            at = pl.multiple_of((zi * 6 + yi) * 96, 32)
            cx[pl.ds(at, 32), 0:128] = odd_b
            cx[pl.ds(at, 32), 128:256] = after_lane(even_b.astype(F32), last).astype(BF)
            cx[pl.ds(at + 32, 32), :] = row
            cx[pl.ds(at + 64, 32), 0:128] = before_lane(odd_b.astype(F32), first).astype(BF)
            cx[pl.ds(at + 64, 32), 128:256] = even_b

    @pl.loop(0, 4)
    def _(zo):
        before = mm(t_bwd[...], cx[pl.ds(pl.multiple_of(zo * 576, 32), 1728), :])
        for yo in range(4):
            grad = jnp.where(
                he[1 + zo, 1 + yo].astype(F32) > 0.0, before[yo * 32 : yo * 32 + 32], 0.0
            )
            gh[1 + zo, 1 + yo] = grad.astype(BF)

    halo_start(*g_halo)

    def spread_grad(row, slot):
        even, odd = row[:, 0:128], row[:, 128:256]
        hgx[slot, 0:32] = before_lane(odd.astype(F32), first).astype(BF)
        hgx[slot, 32:64] = even
        hgx[slot, 64:96] = odd
        hgx[slot, 96:128] = after_lane(even.astype(F32), last).astype(BF)

    for zi in range(1, 5):
        for yi in range(1, 5):
            spread_grad(gh[zi, yi], zi * 6 + yi)

    for sz in range(2):
        for sy in range(2):
            lhs, rhs = [], []
            for jz in (0, 1) if sz else (1, 2):
                for jy in (0, 1) if sy else (1, 2):
                    lhs.append(hgx[(2 * jz + sz) * 6 + 2 * jy + sy])
                    rhs.append(
                        jnp.concatenate(
                            [fh[jz + 1 - vz, jy + 1 - vy] for vz in range(2) for vy in range(2)],
                            axis=0,
                        )
                    )
            grad = mm_nt(jnp.concatenate(lhs, axis=1), jnp.concatenate(rhs, axis=1)).astype(BF)
            at = (sz * 2 + sy) * 256
            part[at : at + 128] = grad[:, 0:128]
            part[at + 128 : at + 256] = grad[:, 128:256]
    part[1024:1536] = jnp.zeros((512, 128), BF)
    for dz in range(3):
        total = jnp.zeros((128, 576), F32)
        for zo in range(4):
            total = total + mm_nt(
                ch[1 + zo, 1:5].reshape(128, 256), hx[(zo + dz) * 576 : (zo + dz + 1) * 576, :]
            )
        for dy in range(3):
            grad = total[0:32, dy * 96 : dy * 96 + 96]
            for yo in range(1, 4):
                grad = grad + total[yo * 32 : yo * 32 + 32, (yo + dy) * 96 : (yo + dy) * 96 + 96]
            at = 1024 + (dz * 3 + dy) * 32
            part[at : at + 32, 0:96] = grad.astype(BF)

    def remote(src, dst, send, recv, device):
        return pltpu.make_async_remote_copy(
            src_ref=src, dst_ref=dst, send_sem=send, recv_sem=recv,
            device_id=device, device_id_type=MESH,
        )

    mine = pl.multiple_of(core * HALF, 16)
    other = pl.multiple_of((1 - core) * HALF, 16)
    copy0 = remote(part.at[pl.ds(other, HALF)], got0, s0_send, s0_recv, partner)
    copy0.start()

    @pl.loop(0, 4)
    def _(zo):
        done = mm(t_fwd[...], hx[pl.ds(pl.multiple_of(zo * 576, 32), 1728), :])
        dec[pl.ds(pl.multiple_of(zo * 128, 16), 128), :] = done.astype(BF)

    copy0.wait()
    pair[...] = (part[pl.ds(mine, HALF), :].astype(F32) + got0[...].astype(F32)).astype(BF)

    def copy1(step):
        q, device = xy_peer(step)
        return remote(
            pair.at[pl.ds(pl.multiple_of(q * PIECE, 16), PIECE)], got1.at[xy],
            s1_send.at[step], s1_recv.at[step], device,
        )

    @pl.loop(1, 16)
    def _(step):
        copy1(step).start()

    got1[xy] = pair[pl.ds(pl.multiple_of(xy * PIECE, 16), PIECE), :]
    joined = mm_nt(dec[...], split).astype(BF)
    order = one_hot(512, 512, lambda r: (r & 15) * 32 + (r >> 4))
    dec_ref[...] = mm(order, joined).astype(BF)

    @pl.loop(1, 16)
    def _(step):
        copy1(step).wait()

    total = got1[0].astype(F32)
    for k in range(1, 16):
        total = total + got1[k].astype(F32)
    got2[chip_z] = total.astype(BF)

    def copy2(step):
        _, device = z_peer(step)
        return remote(
            got2.at[chip_z], got2.at[chip_z], s2_send.at[step], s2_recv.at[step], device
        )

    @pl.loop(1, 8)
    def _(step):
        copy2(step).start()

    halo_arrived(*g_halo)
    for zi in range(6):
        for yi in range(6):
            if zi in (0, 5) or yi in (0, 5):
                spread_grad(gh[zi, yi], zi * 6 + yi)
    back_up = uwt[...].reshape(2048, 64)
    flat = []
    for iz in range(2):
        columns = []
        for iy in range(2):
            columns.append(
                jnp.concatenate(
                    [
                        hgx[(2 * iz + kz) * 6 + 2 * iy + ky]
                        for kz in range(4)
                        for ky in range(4)
                    ],
                    axis=0,
                )
            )
        both = mm_tn(back_up, jnp.concatenate(columns, axis=1)).astype(BF)
        flat += [both[:, 0:128], both[:, 128:256]]
    order = one_hot(256, 256, lambda r: (r & 3) * 64 + (r >> 2))
    fgrad_ref[...] = mm(order, jnp.concatenate(flat, axis=0)).astype(BF)

    @pl.loop(1, 8)
    def _(step):
        copy2(step).wait()

    total = got2[0].astype(F32)
    for k in range(1, 8):
        total = total + got2[k].astype(F32)
    spot = pl.multiple_of(mine + xy * PIECE, 16)
    full[pl.ds(spot, PIECE), :] = total.astype(BF)

    def copy3(step):
        _, device = xy_peer(step)
        here = full.at[pl.ds(spot, PIECE)]
        return remote(here, here, s3_send.at[step], s3_recv.at[step], device)

    @pl.loop(1, 16)
    def _(step):
        copy3(step).start()

    @pl.loop(1, 16)
    def _(step):
        copy3(step).wait()

    here = full.at[pl.ds(mine, HALF)]
    copy4 = remote(here, here, s4_send, s4_recv, partner)
    copy4.start()
    halo_sent(*f_halo)
    halo_sent(*c_halo)
    halo_sent(*g_halo)
    copy4.wait()

    scale = 1.0 / math.sqrt(131072)
    for sz in range(2):
        for vz in range(2):
            for sy in range(2):
                at = ((sz * 2 + sy) * 2 + vz) * 128
                for kx in range(4):
                    rows = full[at + kx * 32 : at + kx * 32 + 32, :].astype(F32) * scale
                    for vy in range(2):
                        k = (2 * vz + sz) * 16 + (2 * vy + sy) * 4 + kx
                        ugrad_ref[pl.ds(k, 32, stride=64), :] = rows[:, vy * 64 : vy * 64 + 64]
    scale = 1.0 / math.sqrt(1048576)
    for k in range(9):
        rows = full[1024 + k * 32 : 1024 + k * 32 + 32, :].astype(F32) * scale
        for dx in range(3):
            at = (k * 3 + dx) * 32
            cgrad_ref[at : at + 32, :] = rows[:, dx * 32 : dx * 32 + 32]


def shards(features, up_weight, conv_weight, out_grad, labels):
    dma = pltpu.SemaphoreType.DMA
    vmem = pltpu.VMEM
    decoded, features_grad, up_grad, conv_grad = pl.pallas_call(
        kernel,
        out_shape=(
            jax.ShapeDtypeStruct((512, 256), BF),
            jax.ShapeDtypeStruct((256, 128), BF),
            jax.ShapeDtypeStruct((2048, 64), F32),
            jax.ShapeDtypeStruct((864, 32), F32),
        ),
        in_specs=[pl.BlockSpec(memory_space=vmem)] * 5,
        out_specs=[pl.BlockSpec(memory_space=vmem)] * 4,
        scratch_shapes=[
            vmem((4, 4, 64, 128), BF),
            vmem((6, 6, 32, 256), BF),
            vmem((6, 6, 32, 256), BF),
            vmem((16, 192, 128), BF),
            vmem((3456, 256), BF),
            vmem((3456, 256), BF),
            vmem((36, 128, 128), BF),
            vmem((6, 6, 32, 256), BF),
            vmem((2048, 64), F32),
            vmem((64, 32, 64), BF),
            vmem((256, 768), BF),
            vmem((128, 1728), BF),
            vmem((128, 1728), BF),
            vmem((512, 256), BF),
            vmem((2 * HALF, 128), BF),
            vmem((HALF, 128), BF),
            vmem((HALF, 128), BF),
            vmem((16, PIECE, 128), BF),
            vmem((8, PIECE, 128), BF),
            vmem((2 * HALF, 128), BF),
            dma((8,)), dma((8,)), dma((8,)), dma((8,)), dma((8,)), dma((8,)),
            dma, dma, dma((16,)), dma((16,)), dma((8,)), dma((8,)), dma((16,)), dma((16,)), dma, dma,
        ],
        compiler_params=pltpu.CompilerParams(
            collective_id=0, has_side_effects=True, vmem_limit_bytes=48 * 1024 * 1024
        ),
        name="decoder_step",
    )(
        features.reshape(256, 128),
        jnp.transpose(up_weight, (1, 2, 3, 4, 0)).reshape(2048, 64),
        jnp.transpose(conv_weight, (2, 3, 4, 0, 1)).reshape(864, 32),
        out_grad.reshape(512, 256),
        labels.reshape(16, 256),
    )
    return (
        decoded.reshape(32, 4, 4, 256),
        features_grad.reshape(64, 2, 2, 128),
        jnp.transpose(up_grad.reshape(32, 4, 4, 4, 64), (4, 0, 1, 2, 3)),
        jnp.transpose(conv_grad.reshape(3, 3, 3, 32, 32), (3, 4, 0, 1, 2)),
    )


def solution(mesh):
    in_specs = (P(None, "gz", "gy", None), P(), P(), P(None, "gz", "gy", None), P("gz", "gy", None))
    out_specs = (P(None, "gz", "gy", None), P(None, "gz", "gy", None), P(), P())
    return jax.shard_map(shards, mesh=mesh, in_specs=in_specs, out_specs=out_specs, check_vma=False)
```

```python
import math

import jax
import jax.numpy as jnp
from jax import lax
from jax.experimental import pallas as pl
from jax.experimental.pallas import tpu as pltpu
from jax.sharding import PartitionSpec as P

BF = jnp.bfloat16
F32 = jnp.float32
MESH = pl.DeviceIdType.MESH

NZ, NY = 8, 32
DIRECTIONS = [(dz, dy) for dz in (-1, 0, 1) for dy in (-1, 0, 1) if (dz, dy) != (0, 0)]
XY_STEPS = sorted(
    [(dx, dy) for dx in range(4) for dy in range(4) if (dx, dy) != (0, 0)],
    key=lambda step: -(min(step[0], 4 - step[0]) + min(step[1], 4 - step[1])),
)
Z_STEPS = (4, 3, 5, 2, 6, 1, 7)
PIECE = 48
HALF = 16 * PIECE


def mm(a, b):
    return lax.dot_general(a, b, (((1,), (0,)), ((), ())), preferred_element_type=F32)


def mm_nt(a, b):
    return lax.dot_general(a, b, (((1,), (1,)), ((), ())), preferred_element_type=F32)


def mm_tn(a, b):
    return lax.dot_general(a, b, (((0,), (0,)), ((), ())), preferred_element_type=F32)


def one_hot(rows, cols, place):
    row = lax.broadcasted_iota(jnp.int32, (rows, cols), 0)
    col = lax.broadcasted_iota(jnp.int32, (rows, cols), 1)
    return jnp.where(place(row) == col, 1.0, 0.0).astype(BF)


def lane_masks(rows):
    lane = lax.broadcasted_iota(jnp.int32, (rows, 128), 1)
    return lane == 0, lane == 127


def before_lane(x, first):
    return jnp.where(first, 0.0, pltpu.roll(x, 1, 1))


def after_lane(x, last):
    return jnp.where(last, 0.0, pltpu.roll(x, 127, 1))


def halo_source(step, extent):
    if step == 0:
        return pl.ds(1, extent)
    return pl.ds(extent, 1) if step == 1 else pl.ds(1, 1)


def halo_target(step, extent):
    if step == 0:
        return pl.ds(1, extent)
    return pl.ds(0, 1) if step == 1 else pl.ds(extent + 1, 1)


def kernel(
    feat_hbm, up_hbm, conv_hbm, og_hbm, lab_hbm,
    dec_ref, fgrad_ref, ugrad_ref, cgrad_ref,
    feat_ref, up_ref, conv_ref, og_ref, lab_ref, load_sem,
    fh, ch, gh, fx, hx, cx, hgx, he,
    upf, uwt, t_up, t_fwd, t_bwd, dec,
    part, got0, pair, got1, got2, full,
    f_send, f_recv, c_send, c_recv, g_send, g_recv,
    s0_send, s0_recv, s1_send, s1_recv, s2_send, s2_recv, s3_send, s3_recv, s4_send, s4_recv,
):
    gz = lax.axis_index("gz")
    gy = lax.axis_index("gy")
    core = gz % 2
    z_lo = gz // 2
    z_hi = gy // 16
    xy = gy % 16
    chip_z = z_hi * 4 + z_lo
    partner = (gz + 1 - 2 * core, gy)

    def xy_peer(step):
        q = (xy // 4 + step[0]) % 4 * 4 + (xy % 4 + step[1]) % 4
        return q, (gz, z_hi * 16 + q)

    def z_peer(step):
        q = (chip_z + step) % 8
        return (q % 4) * 2 + core, (q // 4) * 16 + xy

    def exists(dz, dy):
        return (gz + dz >= 0) & (gz + dz < NZ) & (gy + dy >= 0) & (gy + dy < NY)

    barrier = pltpu.get_barrier_semaphore()
    for dz, dy in DIRECTIONS:
        @pl.when(exists(dz, dy))
        def _():
            pl.semaphore_signal(barrier, 1, device_id=(gz + dz, gy + dy), device_id_type=MESH)

    loads = [
        pltpu.make_async_copy(source, target, load_sem.at[index])
        for index, (source, target) in enumerate(
            (
                (feat_hbm, feat_ref),
                (og_hbm, og_ref),
                (lab_hbm, lab_ref),
                (up_hbm, up_ref),
                (conv_hbm, conv_ref),
            )
        )
    ]
    for load in loads:
        load.start()
    pl.semaphore_signal(barrier, 1, device_id=partner, device_id_type=MESH)

    for step in XY_STEPS:
        pl.semaphore_signal(barrier, 1, device_id=xy_peer(step)[1], device_id_type=MESH)
    for step in Z_STEPS:
        pl.semaphore_signal(barrier, 1, device_id=z_peer(step), device_id_type=MESH)

    loads[0].wait()
    local = mm(one_hot(256, 256, lambda r: (r & 63) * 4 + (r >> 6)), feat_ref[...]).astype(BF)
    for k in range(4):
        fh[1 + k // 2, 1 + k % 2] = local[k * 64 : (k + 1) * 64]

    split = one_hot(256, 256, lambda r: (r & 1) * 128 + (r >> 1))
    loads[1].wait()
    loads[2].wait()
    masked = (og_ref[...].reshape(32, 32, 128) * lab_ref[...].astype(BF)[None]).reshape(1024, 128)
    rows = mm(
        one_hot(512, 512, lambda r: (r & 15) * 32 + (r >> 4)),
        jnp.concatenate([masked[0:512], masked[512:1024]], axis=1),
    ).astype(BF)
    for k in range(16):
        for half in range(2):
            at = ((k // 4) * 8 + half * 4 + k % 4) * 16
            for group in range(2):
                dec[k * 32 + group * 16 : k * 32 + group * 16 + 16, half * 128 : half * 128 + 128] = (
                    rows[at : at + 16, group * 128 : group * 128 + 128]
                )
    local = mm(dec[...], split).astype(BF)
    for k in range(16):
        ch[1 + k // 4, 1 + k % 4] = local[k * 32 : (k + 1) * 32]

    beside = 1 * (gz > 0) + 1 + 1 * (gz < NZ - 1)
    beside = beside * (1 * (gy > 0) + 1 + 1 * (gy < NY - 1)) - 1
    pl.semaphore_wait(barrier, beside + 1 + 15 + 7)

    def halo_copy(buf, extent, index, send, recv):
        dz, dy = DIRECTIONS[index]
        return pltpu.make_async_remote_copy(
            src_ref=buf.at[halo_source(dz, extent), halo_source(dy, extent)],
            dst_ref=buf.at[halo_target(dz, extent), halo_target(dy, extent)],
            send_sem=send.at[index],
            recv_sem=recv.at[index],
            device_id=(gz + dz, gy + dy),
            device_id_type=MESH,
        )

    def halo_start(*what):
        for index, (dz, dy) in enumerate(DIRECTIONS):
            @pl.when(exists(dz, dy))
            def _():
                halo_copy(what[0], what[1], index, what[2], what[3]).start()

    def halo_arrived(*what):
        for index, (dz, dy) in enumerate(DIRECTIONS):
            @pl.when(exists(-dz, -dy))
            def _():
                halo_copy(what[0], what[1], index, what[2], what[3]).wait_recv()

    def halo_sent(*what):
        for index, (dz, dy) in enumerate(DIRECTIONS):
            @pl.when(exists(dz, dy))
            def _():
                halo_copy(what[0], what[1], index, what[2], what[3]).wait_send()

    f_halo = (fh, 2, f_send, f_recv)
    c_halo = (ch, 4, c_send, c_recv)
    g_halo = (gh, 4, g_send, g_recv)
    halo_start(*f_halo)
    halo_start(*c_halo)

    @pl.when(gz == 0)
    def _():
        for buf in (fh, ch, gh):
            buf[0] = jnp.zeros(buf.shape[1:], BF)

    @pl.when(gz == NZ - 1)
    def _():
        for buf in (fh, ch, gh):
            buf[buf.shape[0] - 1] = jnp.zeros(buf.shape[1:], BF)

    @pl.when(gy == 0)
    def _():
        for buf in (fh, ch, gh):
            for k in range(buf.shape[0]):
                buf[k, 0] = jnp.zeros(buf.shape[2:], BF)

    @pl.when(gy == NY - 1)
    def _():
        for buf in (fh, ch, gh):
            for k in range(buf.shape[0]):
                buf[k, buf.shape[1] - 1] = jnp.zeros(buf.shape[2:], BF)

    loads[3].wait()
    loads[4].wait()
    upf[...] = up_ref[...].astype(F32)

    @pl.loop(0, 64)
    def _(k):
        uwt[k] = upf[pl.ds(k, 32, stride=64), :].astype(BF)

    for sz in range(2):
        for sy in range(2):
            for px in range(2):
                blocks = []
                for uz in range(2):
                    for uy in range(2):
                        base = (2 * (1 - uz) + sz) * 16 + (2 * (1 - uy) + sy) * 4
                        none = jnp.zeros((32, 64), BF)
                        if px == 0:
                            blocks += [uwt[base + 3], uwt[base + 1], none]
                        else:
                            blocks += [none, uwt[base + 2], uwt[base]]
                at = ((sz * 2 + sy) * 2 + px) * 32
                t_up[at : at + 32, :] = jnp.concatenate(blocks, axis=1)
    zero = jnp.zeros((32, 96), BF)
    taps = {}
    back = {}
    for dz in range(3):
        for dy in range(3):
            at = (dz * 3 + dy) * 96
            taps[dz, dy] = jnp.concatenate(
                [conv_ref[at + 32 * dx : at + 32 * dx + 32, :] for dx in range(3)], axis=1
            )
            back[2 - dz, 2 - dy] = conv_ref[at : at + 96, :].T
    for yo in range(4):
        for matrix, source in ((t_fwd, taps), (t_bwd, back)):
            matrix[yo * 32 : yo * 32 + 32, :] = jnp.concatenate(
                [
                    source[dz, yi - yo] if 0 <= yi - yo < 3 else zero
                    for dz in range(3)
                    for yi in range(6)
                ],
                axis=1,
            )

    first64, last64 = lane_masks(64)
    first, last = lane_masks(32)

    def spread_cotangent(zi, yi):
        row = ch[zi, yi]
        even, odd = row[:, 0:128], row[:, 128:256]
        at = (zi * 6 + yi) * 96
        cx[at : at + 32, 0:128] = odd
        cx[at : at + 32, 128:256] = after_lane(even.astype(F32), last).astype(BF)
        cx[at + 32 : at + 64, :] = row
        cx[at + 64 : at + 96, 0:128] = before_lane(odd.astype(F32), first).astype(BF)
        cx[at + 64 : at + 96, 128:256] = even

    for zi in range(1, 5):
        for yi in range(1, 5):
            spread_cotangent(zi, yi)

    halo_arrived(*f_halo)
    for k in range(16):
        row = fh[k // 4, k % 4]
        wide = row.astype(F32)
        fx[k, 0:64] = before_lane(wide, first64).astype(BF)
        fx[k, 64:128] = row
        fx[k, 128:192] = after_lane(wide, last64).astype(BF)

    @pl.loop(0, 3)
    def _(jz):
        columns = []
        for jy in range(3):
            columns.append(
                jnp.concatenate(
                    [fx[(jz + uz) * 4 + jy + uy] for uz in range(2) for uy in range(2)], axis=0
                )
            )
        lifted = jnp.maximum(mm(t_up[...], jnp.concatenate(columns, axis=1)), 0.0)
        for sz in range(2):
            for sy in range(2):
                for jy in range(3):
                    at = (sz * 2 + sy) * 64
                    even = lifted[at : at + 32, jy * 128 : jy * 128 + 128]
                    odd = lifted[at + 32 : at + 64, jy * 128 : jy * 128 + 128]
                    zo, yo = jz * 2 + sz, jy * 2 + sy
                    at = pl.multiple_of((zo * 6 + yo) * 96, 32)
                    even_b, odd_b = even.astype(BF), odd.astype(BF)
                    hx[pl.ds(at, 32), 0:128] = before_lane(odd, first).astype(BF)
                    hx[pl.ds(at, 32), 128:256] = even_b
                    hx[pl.ds(at + 32, 32), 0:128] = even_b
                    hx[pl.ds(at + 32, 32), 128:256] = odd_b
                    hx[pl.ds(at + 64, 32), 0:128] = odd_b
                    hx[pl.ds(at + 64, 32), 128:256] = after_lane(even, last).astype(BF)
                    he[zo, yo, :, 0:128] = even_b
                    he[zo, yo, :, 128:256] = odd_b

    @pl.when(gz == 0)
    def _():
        hx[0:576] = jnp.zeros((576, 256), BF)

    @pl.when(gz == NZ - 1)
    def _():
        hx[2880:3456] = jnp.zeros((576, 256), BF)

    @pl.when(gy == 0)
    def _():
        for zi in range(6):
            hx[zi * 576 : zi * 576 + 96] = jnp.zeros((96, 256), BF)

    @pl.when(gy == NY - 1)
    def _():
        for zi in range(6):
            hx[zi * 576 + 480 : zi * 576 + 576] = jnp.zeros((96, 256), BF)

    halo_arrived(*c_halo)
    for zi in range(6):
        for yi in range(6):
            if zi in (0, 5) or yi in (0, 5):
                spread_cotangent(zi, yi)

    @pl.loop(0, 4)
    def _(zo):
        before = mm(t_bwd[...], cx[pl.ds(pl.multiple_of(zo * 576, 32), 1728), :])
        for yo in range(4):
            grad = jnp.where(
                he[1 + zo, 1 + yo].astype(F32) > 0.0, before[yo * 32 : yo * 32 + 32], 0.0
            )
            gh[1 + zo, 1 + yo] = grad.astype(BF)

    halo_start(*g_halo)

    def spread_grad(row, slot):
        even, odd = row[:, 0:128], row[:, 128:256]
        hgx[slot, 0:32] = before_lane(odd.astype(F32), first).astype(BF)
        hgx[slot, 32:64] = even
        hgx[slot, 64:96] = odd
        hgx[slot, 96:128] = after_lane(even.astype(F32), last).astype(BF)

    for zi in range(1, 5):
        for yi in range(1, 5):
            spread_grad(gh[zi, yi], zi * 6 + yi)

    for sz in range(2):
        for sy in range(2):
            lhs, rhs = [], []
            for jz in (0, 1) if sz else (1, 2):
                for jy in (0, 1) if sy else (1, 2):
                    lhs.append(hgx[(2 * jz + sz) * 6 + 2 * jy + sy])
                    rhs.append(
                        jnp.concatenate(
                            [fh[jz + 1 - vz, jy + 1 - vy] for vz in range(2) for vy in range(2)],
                            axis=0,
                        )
                    )
            grad = mm_nt(jnp.concatenate(lhs, axis=1), jnp.concatenate(rhs, axis=1)).astype(BF)
            at = sz * HALF + sy * 256
            part[at : at + 128] = grad[:, 0:128]
            part[at + 128 : at + 256] = grad[:, 128:256]
    for half in range(2):
        part[half * HALF + 512 : (half + 1) * HALF] = jnp.zeros((HALF - 512, 128), BF)
    for dz in range(3):
        total = jnp.zeros((128, 576), F32)
        for zo in range(4):
            total = total + mm_nt(
                ch[1 + zo, 1:5].reshape(128, 256), hx[(zo + dz) * 576 : (zo + dz + 1) * 576, :]
            )
        for dy in range(3):
            grad = total[0:32, dy * 96 : dy * 96 + 96]
            for yo in range(1, 4):
                grad = grad + total[yo * 32 : yo * 32 + 32, (yo + dy) * 96 : (yo + dy) * 96 + 96]
            for half in range(2):
                if 0 <= dz * 3 + dy - 4 * half < 5:
                    at = half * HALF + 512 + (dz * 3 + dy - 4 * half) * 32
                    part[at : at + 32, 0:96] = grad.astype(BF)

    def remote(src, dst, send, recv, device):
        return pltpu.make_async_remote_copy(
            src_ref=src, dst_ref=dst, send_sem=send, recv_sem=recv,
            device_id=device, device_id_type=MESH,
        )

    mine = pl.multiple_of(core * HALF, 16)
    other = pl.multiple_of((1 - core) * HALF, 16)
    copy0 = remote(part.at[pl.ds(other, HALF)], got0, s0_send, s0_recv, partner)
    copy0.start()

    copy0.wait()
    pair[...] = (part[pl.ds(mine, HALF), :].astype(F32) + got0[...].astype(F32)).astype(BF)

    for index, step in enumerate(XY_STEPS):
        q, device = xy_peer(step)
        remote(
            pair.at[pl.ds(pl.multiple_of(q * PIECE, 16), PIECE)], got1.at[index],
            s1_send, s1_recv, device,
        ).start()

    @pl.loop(0, 4)
    def _(zo):
        done = mm(t_fwd[...], hx[pl.ds(pl.multiple_of(zo * 576, 32), 1728), :])
        dec[pl.ds(pl.multiple_of(zo * 128, 16), 128), :] = done.astype(BF)

    joined = mm_nt(dec[...], split).astype(BF)
    blocks = []
    for k in range(32):
        at = ((k // 8) * 4 + k % 4) * 32
        half = (k // 4) % 2 * 128
        blocks.append(
            jnp.concatenate(
                [joined[at : at + 16, half : half + 128], joined[at + 16 : at + 32, half : half + 128]],
                axis=1,
            )
        )
    ordered = mm(
        one_hot(512, 512, lambda r: (r & 31) * 16 + (r >> 5)), jnp.concatenate(blocks, axis=0)
    ).astype(BF)
    dec_ref[0:512] = ordered[:, 0:128]
    dec_ref[512:1024] = ordered[:, 128:256]

    remote(got1, got1, s1_send, s1_recv, partner).wait_recv()
    total = pair[pl.ds(pl.multiple_of(xy * PIECE, 16), PIECE), :].astype(F32)
    for k in range(15):
        total = total + got1[k].astype(F32)
    got2[chip_z] = total.astype(BF)

    here = got2.at[chip_z]
    for step in Z_STEPS:
        remote(here, here, s2_send, s2_recv, z_peer(step)).start()

    seven = got2.at[0:7]
    remote(seven, seven, s2_send, s2_recv, partner).wait_recv()

    total = got2[0].astype(F32)
    for k in range(1, 8):
        total = total + got2[k].astype(F32)
    spot = pl.multiple_of(mine + xy * PIECE, 16)
    full[pl.ds(spot, PIECE), :] = total.astype(BF)

    def pass_on(q):
        here = full.at[pl.ds(pl.multiple_of(mine + q * PIECE, 16), PIECE)]
        remote(here, here, s4_send, s4_recv, partner).start()

    here = full.at[pl.ds(spot, PIECE)]
    for index, step in enumerate(XY_STEPS):
        remote(here, here, s3_send, s3_recv.at[index], xy_peer(step)[1]).start()
    pass_on(xy)

    halo_arrived(*g_halo)
    for zi in range(6):
        for yi in range(6):
            if zi in (0, 5) or yi in (0, 5):
                spread_grad(gh[zi, yi], zi * 6 + yi)
    back_up = uwt[...].reshape(2048, 64)
    flat = []
    for iz in range(2):
        columns = []
        for iy in range(2):
            columns.append(
                jnp.concatenate(
                    [
                        hgx[(2 * iz + kz) * 6 + 2 * iy + ky]
                        for kz in range(4)
                        for ky in range(4)
                    ],
                    axis=0,
                )
            )
        both = mm_tn(back_up, jnp.concatenate(columns, axis=1)).astype(BF)
        flat += [both[:, 0:128], both[:, 128:256]]
    order = one_hot(256, 256, lambda r: (r & 3) * 64 + (r >> 2))
    fgrad_ref[...] = mm(order, jnp.concatenate(flat, axis=0)).astype(BF)

    for index in reversed(range(15)):
        dx, dy = XY_STEPS[index]
        remote(here, here, s3_send, s3_recv.at[index], partner).wait_recv()
        pass_on(xy_peer((-dx, -dy))[0])

    halo_sent(*f_halo)
    halo_sent(*c_halo)
    halo_sent(*g_halo)
    remote(got1, got1, s1_send, s1_recv, partner).wait_send()
    remote(seven, seven, s2_send, s2_recv, partner).wait_send()
    remote(got1, got1, s3_send, s1_recv, partner).wait_send()
    def convert(half):
        start = pl.multiple_of(half * HALF, 16)
        scale = 1.0 / math.sqrt(131072)
        for unit in range(16):
            sy, vz, kx = unit // 8, unit // 4 % 2, unit % 4
            rows = full[pl.ds(start + unit * 32, 32), :].astype(F32) * scale
            for vy in range(2):
                k = half * 16 + vz * 32 + (2 * vy + sy) * 4 + kx
                ugrad_ref[pl.ds(k, 32, stride=64), :] = rows[:, vy * 64 : vy * 64 + 64]
        scale = 1.0 / math.sqrt(1048576)
        for unit in range(5):
            rows = full[pl.ds(start + 512 + unit * 32, 32), :].astype(F32) * scale
            for dx in range(3):
                at = pl.multiple_of(half * 384 + (unit * 3 + dx) * 32, 8)
                cgrad_ref[pl.ds(at, 32), :] = rows[:, dx * 32 : dx * 32 + 32]

    convert(core)
    here = full.at[pl.ds(mine, HALF)]
    remote(here, here, s4_send, s4_recv, partner).wait()

    convert(1 - core)


def write_out(*refs):
    sources, targets, sem = refs[0:4], refs[4:8], refs[8]
    copies = [pltpu.make_async_copy(sources[k], targets[k], sem.at[k]) for k in range(4)]
    for copy in copies:
        copy.start()
    for copy in copies:
        copy.wait()


def in_hbm(x):
    return pltpu.with_memory_space_constraint(x, pltpu.HBM)


def shards(features, up_weight, conv_weight, out_grad, labels):
    dma = pltpu.SemaphoreType.DMA
    vmem = pltpu.VMEM
    shapes = (
        jax.ShapeDtypeStruct((1024, 128), BF),
        jax.ShapeDtypeStruct((256, 128), BF),
        jax.ShapeDtypeStruct((2048, 64), F32),
        jax.ShapeDtypeStruct((864, 32), F32),
    )
    results = pl.pallas_call(
        kernel,
        out_shape=tuple(vmem(shape.shape, shape.dtype) for shape in shapes),
        in_specs=[pl.BlockSpec(memory_space=pl.ANY)] * 5,
        out_specs=[pl.BlockSpec(memory_space=vmem)] * 4,
        scratch_shapes=[
            vmem((256, 128), BF),
            vmem((2048, 64), BF),
            vmem((864, 32), BF),
            vmem((1024, 128), BF),
            vmem((32, 128), jnp.int32),
            dma((5,)),
            vmem((4, 4, 64, 128), BF),
            vmem((6, 6, 32, 256), BF),
            vmem((6, 6, 32, 256), BF),
            vmem((16, 192, 128), BF),
            vmem((3456, 256), BF),
            vmem((3456, 256), BF),
            vmem((36, 128, 128), BF),
            vmem((6, 6, 32, 256), BF),
            vmem((2048, 64), F32),
            vmem((64, 32, 64), BF),
            vmem((256, 768), BF),
            vmem((128, 1728), BF),
            vmem((128, 1728), BF),
            vmem((512, 256), BF),
            vmem((2 * HALF, 128), BF),
            vmem((HALF, 128), BF),
            vmem((HALF, 128), BF),
            vmem((15, PIECE, 128), BF),
            vmem((8, PIECE, 128), BF),
            vmem((2 * HALF, 128), BF),
            dma((8,)), dma((8,)), dma((8,)), dma((8,)), dma((8,)), dma((8,)),
            dma, dma, dma, dma, dma, dma, dma, dma((16,)), dma, dma,
        ],
        compiler_params=pltpu.CompilerParams(
            collective_id=0, has_side_effects=True, vmem_limit_bytes=40 * 1024 * 1024
        ),
        name="decoder_step",
    )(
        in_hbm(features.reshape(256, 128)),
        in_hbm(jnp.transpose(up_weight, (1, 2, 3, 4, 0)).reshape(2048, 64)),
        in_hbm(jnp.transpose(conv_weight, (2, 3, 4, 0, 1)).reshape(864, 32)),
        in_hbm(jnp.transpose(out_grad.reshape(32, 4, 4, 2, 128), (0, 1, 3, 2, 4)).reshape(1024, 128)),
        in_hbm(jnp.transpose(labels.reshape(4, 4, 2, 128), (0, 2, 1, 3)).reshape(32, 128)),
    )
    decoded, features_grad, up_grad, conv_grad = pl.pallas_call(
        write_out,
        out_shape=shapes,
        in_specs=[pl.BlockSpec(memory_space=pl.ANY)] * 4,
        out_specs=[pl.BlockSpec(memory_space=pl.ANY)] * 4,
        scratch_shapes=[dma((4,))],
        compiler_params=pltpu.CompilerParams(vmem_limit_bytes=40 * 1024 * 1024),
        name="write_out",
    )(*results)
    return (
        jnp.transpose(decoded.reshape(32, 4, 2, 4, 128), (0, 1, 3, 2, 4)).reshape(32, 4, 4, 256),
        features_grad.reshape(64, 2, 2, 128),
        jnp.transpose(up_grad.reshape(32, 4, 4, 4, 64), (4, 0, 1, 2, 3)),
        jnp.transpose(conv_grad.reshape(3, 3, 3, 32, 32), (3, 4, 0, 1, 2)),
    )


def solution(mesh):
    in_specs = (P(None, "gz", "gy", None), P(), P(), P(None, "gz", "gy", None), P("gz", "gy", None))
    out_specs = (P(None, "gz", "gy", None), P(None, "gz", "gy", None), P(), P())
    return jax.shard_map(shards, mesh=mesh, in_specs=in_specs, out_specs=out_specs, check_vma=False)
```

```python
import math

import jax
import jax.numpy as jnp
from jax import lax
from jax.experimental import pallas as pl
from jax.experimental.pallas import tpu as pltpu
from jax.sharding import PartitionSpec as P

BF = jnp.bfloat16
F32 = jnp.float32
MESH = pl.DeviceIdType.MESH

NZ, NY = 8, 32
DIRECTIONS = [(dz, dy) for dz in (-1, 0, 1) for dy in (-1, 0, 1) if (dz, dy) != (0, 0)]
XY_STEPS = sorted(
    [(dx, dy) for dx in range(4) for dy in range(4) if (dx, dy) != (0, 0)],
    key=lambda step: -(min(step[0], 4 - step[0]) + min(step[1], 4 - step[1])),
)
Z_STEPS = (4, 3, 5, 2, 6, 1, 7)
PIECE = 48
HALF = 16 * PIECE


def mm(a, b):
    return lax.dot_general(a, b, (((1,), (0,)), ((), ())), preferred_element_type=F32)


def mm_nt(a, b):
    return lax.dot_general(a, b, (((1,), (1,)), ((), ())), preferred_element_type=F32)


def mm_tn(a, b):
    return lax.dot_general(a, b, (((0,), (0,)), ((), ())), preferred_element_type=F32)


def one_hot(rows, cols, place):
    row = lax.broadcasted_iota(jnp.int32, (rows, cols), 0)
    col = lax.broadcasted_iota(jnp.int32, (rows, cols), 1)
    return jnp.where(place(row) == col, 1.0, 0.0).astype(BF)


def lane_masks(rows):
    lane = lax.broadcasted_iota(jnp.int32, (rows, 128), 1)
    return lane == 0, lane == 127


def before_lane(x, first):
    return jnp.where(first, 0.0, pltpu.roll(x, 1, 1))


def after_lane(x, last):
    return jnp.where(last, 0.0, pltpu.roll(x, 127, 1))


def halo_source(step, extent):
    if step == 0:
        return pl.ds(1, extent)
    return pl.ds(extent, 1) if step == 1 else pl.ds(1, 1)


def halo_target(step, extent):
    if step == 0:
        return pl.ds(1, extent)
    return pl.ds(0, 1) if step == 1 else pl.ds(extent + 1, 1)


def kernel(
    feat_hbm, up_hbm, conv_hbm, og_hbm, lab_hbm,
    dec_ref, fgrad_ref, ugrad_ref, cgrad_ref,
    feat_ref, up_ref, conv_ref, og_ref, lab_ref, load_sem,
    fh, ch, gh, fx, hx, cx, hgx, he,
    upf, uwt, t_up, t_fwd, t_bwd, dec,
    part, got0, pair, got1, got2, full,
    f_send, f_recv, c_send, c_recv, g_send, g_recv,
    s0_send, s0_recv, s1_send, s1_recv, s2_send, s2_recv, s3_send, s3_recv, s4_send, s4_recv,
):
    gz = lax.axis_index("gz")
    gy = lax.axis_index("gy")
    core = gz % 2
    z_lo = gz // 2
    z_hi = gy // 16
    xy = gy % 16
    chip_z = z_hi * 4 + z_lo
    partner = (gz + 1 - 2 * core, gy)

    def xy_peer(step):
        q = (xy // 4 + step[0]) % 4 * 4 + (xy % 4 + step[1]) % 4
        return q, (gz, z_hi * 16 + q)

    def z_peer(step):
        q = (chip_z + step) % 8
        return (q % 4) * 2 + core, (q // 4) * 16 + xy

    def exists(dz, dy):
        return (gz + dz >= 0) & (gz + dz < NZ) & (gy + dy >= 0) & (gy + dy < NY)

    barrier = pltpu.get_barrier_semaphore()
    for dz, dy in DIRECTIONS:
        @pl.when(exists(dz, dy))
        def _():
            pl.semaphore_signal(barrier, 1, device_id=(gz + dz, gy + dy), device_id_type=MESH)

    loads = [
        pltpu.make_async_copy(source, target, load_sem.at[index])
        for index, (source, target) in enumerate(
            (
                (feat_hbm, feat_ref),
                (og_hbm, og_ref),
                (lab_hbm, lab_ref),
                (up_hbm, up_ref),
                (conv_hbm, conv_ref),
            )
        )
    ]
    for load in loads:
        load.start()
    pl.semaphore_signal(barrier, 1, device_id=partner, device_id_type=MESH)

    for step in XY_STEPS:
        pl.semaphore_signal(barrier, 1, device_id=xy_peer(step)[1], device_id_type=MESH)
    for step in Z_STEPS:
        pl.semaphore_signal(barrier, 1, device_id=z_peer(step), device_id_type=MESH)

    loads[0].wait()
    local = mm(one_hot(256, 256, lambda r: (r & 63) * 4 + (r >> 6)), feat_ref[...]).astype(BF)
    for k in range(4):
        fh[1 + k // 2, 1 + k % 2] = local[k * 64 : (k + 1) * 64]

    split = one_hot(256, 256, lambda r: (r & 1) * 128 + (r >> 1))
    loads[1].wait()
    loads[2].wait()
    masked = (og_ref[...].reshape(32, 32, 128) * lab_ref[...].astype(BF)[None]).reshape(1024, 128)
    rows = mm(
        one_hot(512, 512, lambda r: (r & 15) * 32 + (r >> 4)),
        jnp.concatenate([masked[0:512], masked[512:1024]], axis=1),
    ).astype(BF)
    for k in range(16):
        for half in range(2):
            at = ((k // 4) * 8 + half * 4 + k % 4) * 16
            for group in range(2):
                dec[k * 32 + group * 16 : k * 32 + group * 16 + 16, half * 128 : half * 128 + 128] = (
                    rows[at : at + 16, group * 128 : group * 128 + 128]
                )
    local = mm(dec[...], split).astype(BF)
    for k in range(16):
        ch[1 + k // 4, 1 + k % 4] = local[k * 32 : (k + 1) * 32]

    beside = 1 * (gz > 0) + 1 + 1 * (gz < NZ - 1)
    beside = beside * (1 * (gy > 0) + 1 + 1 * (gy < NY - 1)) - 1
    pl.semaphore_wait(barrier, beside + 1 + 15 + 7)

    def halo_copy(buf, extent, index, send, recv):
        dz, dy = DIRECTIONS[index]
        return pltpu.make_async_remote_copy(
            src_ref=buf.at[halo_source(dz, extent), halo_source(dy, extent)],
            dst_ref=buf.at[halo_target(dz, extent), halo_target(dy, extent)],
            send_sem=send.at[index],
            recv_sem=recv.at[index],
            device_id=(gz + dz, gy + dy),
            device_id_type=MESH,
        )

    def halo_start(side, *halos):
        for what in halos:
            for index, (dz, dy) in sorted(enumerate(DIRECTIONS), key=lambda item: abs(item[1][0])):
                if dy == side:
                    @pl.when(exists(dz, dy))
                    def _():
                        halo_copy(what[0], what[1], index, what[2], what[3]).start()

    def halo_start_all(*halos):
        @pl.when(gy % 16 == 0)
        def _():
            halo_start(-1, *halos)

        halo_start(1, *halos)
        halo_start(0, *halos)

        @pl.when(gy % 16 > 0)
        def _():
            halo_start(-1, *halos)

    def halo_arrived(*what):
        for index, (dz, dy) in enumerate(DIRECTIONS):
            @pl.when(exists(-dz, -dy))
            def _():
                halo_copy(what[0], what[1], index, what[2], what[3]).wait_recv()

    def halo_sent(*what):
        for index, (dz, dy) in enumerate(DIRECTIONS):
            @pl.when(exists(dz, dy))
            def _():
                halo_copy(what[0], what[1], index, what[2], what[3]).wait_send()

    f_halo = (fh, 2, f_send, f_recv)
    c_halo = (ch, 4, c_send, c_recv)
    g_halo = (gh, 4, g_send, g_recv)
    halo_start_all(f_halo, c_halo)

    @pl.when(gz == 0)
    def _():
        for buf in (fh, ch, gh):
            buf[0] = jnp.zeros(buf.shape[1:], BF)

    @pl.when(gz == NZ - 1)
    def _():
        for buf in (fh, ch, gh):
            buf[buf.shape[0] - 1] = jnp.zeros(buf.shape[1:], BF)

    @pl.when(gy == 0)
    def _():
        for buf in (fh, ch, gh):
            for k in range(buf.shape[0]):
                buf[k, 0] = jnp.zeros(buf.shape[2:], BF)

    @pl.when(gy == NY - 1)
    def _():
        for buf in (fh, ch, gh):
            for k in range(buf.shape[0]):
                buf[k, buf.shape[1] - 1] = jnp.zeros(buf.shape[2:], BF)

    loads[3].wait()
    loads[4].wait()
    upf[...] = up_ref[...].astype(F32)

    @pl.loop(0, 64)
    def _(k):
        uwt[k] = upf[pl.ds(k, 32, stride=64), :].astype(BF)

    for sz in range(2):
        for sy in range(2):
            for px in range(2):
                blocks = []
                for uz in range(2):
                    for uy in range(2):
                        base = (2 * (1 - uz) + sz) * 16 + (2 * (1 - uy) + sy) * 4
                        none = jnp.zeros((32, 64), BF)
                        if px == 0:
                            blocks += [uwt[base + 3], uwt[base + 1], none]
                        else:
                            blocks += [none, uwt[base + 2], uwt[base]]
                at = ((sz * 2 + sy) * 2 + px) * 32
                t_up[at : at + 32, :] = jnp.concatenate(blocks, axis=1)
    zero = jnp.zeros((32, 96), BF)
    taps = {}
    back = {}
    for dz in range(3):
        for dy in range(3):
            at = (dz * 3 + dy) * 96
            taps[dz, dy] = jnp.concatenate(
                [conv_ref[at + 32 * dx : at + 32 * dx + 32, :] for dx in range(3)], axis=1
            )
            back[2 - dz, 2 - dy] = conv_ref[at : at + 96, :].T
    for yo in range(4):
        for matrix, source in ((t_fwd, taps), (t_bwd, back)):
            matrix[yo * 32 : yo * 32 + 32, :] = jnp.concatenate(
                [
                    source[dz, yi - yo] if 0 <= yi - yo < 3 else zero
                    for dz in range(3)
                    for yi in range(6)
                ],
                axis=1,
            )

    first64, last64 = lane_masks(64)
    first, last = lane_masks(32)

    def spread_cotangent(zi, yi):
        row = ch[zi, yi]
        even, odd = row[:, 0:128], row[:, 128:256]
        at = (zi * 6 + yi) * 96
        cx[at : at + 32, 0:128] = odd
        cx[at : at + 32, 128:256] = after_lane(even.astype(F32), last).astype(BF)
        cx[at + 32 : at + 64, :] = row
        cx[at + 64 : at + 96, 0:128] = before_lane(odd.astype(F32), first).astype(BF)
        cx[at + 64 : at + 96, 128:256] = even

    for zi in range(1, 5):
        for yi in range(1, 5):
            spread_cotangent(zi, yi)

    halo_arrived(*f_halo)
    for k in range(16):
        row = fh[k // 4, k % 4]
        wide = row.astype(F32)
        fx[k, 0:64] = before_lane(wide, first64).astype(BF)
        fx[k, 64:128] = row
        fx[k, 128:192] = after_lane(wide, last64).astype(BF)

    for jz in range(3):
        columns = []
        for jy in range(3):
            columns.append(
                jnp.concatenate(
                    [fx[(jz + uz) * 4 + jy + uy] for uz in range(2) for uy in range(2)], axis=0
                )
            )
        lifted = jnp.maximum(mm(t_up[...], jnp.concatenate(columns, axis=1)), 0.0)
        for sz in range(2):
            for sy in range(2):
                for jy in range(3):
                    at = (sz * 2 + sy) * 64
                    even = lifted[at : at + 32, jy * 128 : jy * 128 + 128]
                    odd = lifted[at + 32 : at + 64, jy * 128 : jy * 128 + 128]
                    zo, yo = jz * 2 + sz, jy * 2 + sy
                    at = (zo * 6 + yo) * 96
                    even_b, odd_b = even.astype(BF), odd.astype(BF)
                    hx[pl.ds(at, 32), 0:128] = before_lane(odd, first).astype(BF)
                    hx[pl.ds(at, 32), 128:256] = even_b
                    hx[pl.ds(at + 32, 32), 0:128] = even_b
                    hx[pl.ds(at + 32, 32), 128:256] = odd_b
                    hx[pl.ds(at + 64, 32), 0:128] = odd_b
                    hx[pl.ds(at + 64, 32), 128:256] = after_lane(even, last).astype(BF)
                    he[zo, yo, :, 0:128] = even_b
                    he[zo, yo, :, 128:256] = odd_b

    @pl.when(gz == 0)
    def _():
        hx[0:576] = jnp.zeros((576, 256), BF)

    @pl.when(gz == NZ - 1)
    def _():
        hx[2880:3456] = jnp.zeros((576, 256), BF)

    @pl.when(gy == 0)
    def _():
        for zi in range(6):
            hx[zi * 576 : zi * 576 + 96] = jnp.zeros((96, 256), BF)

    @pl.when(gy == NY - 1)
    def _():
        for zi in range(6):
            hx[zi * 576 + 480 : zi * 576 + 576] = jnp.zeros((96, 256), BF)

    def remote(src, dst, send, recv, device):
        return pltpu.make_async_remote_copy(
            src_ref=src, dst_ref=dst, send_sem=send, recv_sem=recv,
            device_id=device, device_id_type=MESH,
        )

    mine = pl.multiple_of(core * HALF, 16)
    other = pl.multiple_of((1 - core) * HALF, 16)
    for half in range(2):
        part[half * HALF + 512 : (half + 1) * HALF] = jnp.zeros((HALF - 512, 128), BF)
    for dz in range(3):
        total = mm_nt(
            jnp.concatenate([hx[(zo + dz) * 576 : (zo + dz + 1) * 576, :] for zo in range(4)], axis=1),
            jnp.concatenate([ch[1 + zo, 1:5].reshape(128, 256) for zo in range(4)], axis=1),
        )
        for dy in range(3):
            grad = total[dy * 96 : dy * 96 + 96, 0:32]
            for yo in range(1, 4):
                grad = grad + total[(yo + dy) * 96 : (yo + dy) * 96 + 96, yo * 32 : yo * 32 + 32]
            grad = grad.T
            for half in range(2):
                if 0 <= dz * 3 + dy - 4 * half < 5:
                    at = half * HALF + 512 + (dz * 3 + dy - 4 * half) * 32
                    part[at : at + 32, 0:96] = grad.astype(BF)

    copy_conv = remote(
        part.at[pl.ds(pl.multiple_of(other + 512, 16), 256)], got0.at[512:768],
        s0_send.at[0], s0_recv.at[0], partner,
    )
    copy_conv.start()

    halo_arrived(*c_halo)
    for zi in range(6):
        for yi in range(6):
            if zi in (0, 5) or yi in (0, 5):
                spread_cotangent(zi, yi)

    for zo in range(4):
        before = mm(t_bwd[...], cx[pl.ds(zo * 576, 1728), :])
        for yo in range(4):
            grad = jnp.where(
                he[1 + zo, 1 + yo].astype(F32) > 0.0, before[yo * 32 : yo * 32 + 32], 0.0
            )
            gh[1 + zo, 1 + yo] = grad.astype(BF)

    halo_start_all(g_halo)

    def spread_grad(row, slot):
        even, odd = row[:, 0:128], row[:, 128:256]
        hgx[slot, 0:32] = before_lane(odd.astype(F32), first).astype(BF)
        hgx[slot, 32:64] = even
        hgx[slot, 64:96] = odd
        hgx[slot, 96:128] = after_lane(even.astype(F32), last).astype(BF)

    for zi in range(1, 5):
        for yi in range(1, 5):
            spread_grad(gh[zi, yi], zi * 6 + yi)

    for sz in range(2):
        for sy in range(2):
            lhs, rhs = [], []
            for jz in (0, 1) if sz else (1, 2):
                for jy in (0, 1) if sy else (1, 2):
                    lhs.append(hgx[(2 * jz + sz) * 6 + 2 * jy + sy])
                    rhs.append(
                        jnp.concatenate(
                            [fh[jz + 1 - vz, jy + 1 - vy] for vz in range(2) for vy in range(2)],
                            axis=0,
                        )
                    )
            grad = mm_nt(jnp.concatenate(lhs, axis=1), jnp.concatenate(rhs, axis=1)).astype(BF)
            at = sz * HALF + sy * 256
            part[at : at + 128] = grad[:, 0:128]
            part[at + 128 : at + 256] = grad[:, 128:256]
    copy_up = remote(
        part.at[pl.ds(other, 512)], got0.at[0:512], s0_send.at[1], s0_recv.at[1], partner
    )
    copy_up.start()

    copy_conv.wait()
    copy_up.wait()
    pair[...] = (part[pl.ds(mine, HALF), :].astype(F32) + got0[...].astype(F32)).astype(BF)

    for index, step in enumerate(XY_STEPS):
        q, device = xy_peer(step)
        remote(
            pair.at[pl.ds(pl.multiple_of(q * PIECE, 16), PIECE)], got1.at[index],
            s1_send, s1_recv, device,
        ).start()

    for zo in range(4):
        done = mm(t_fwd[...], hx[pl.ds(zo * 576, 1728), :])
        dec[pl.ds(zo * 128, 128), :] = done.astype(BF)

    joined = mm_nt(dec[...], split).astype(BF)
    blocks = []
    for k in range(32):
        at = ((k // 8) * 4 + k % 4) * 32
        half = (k // 4) % 2 * 128
        blocks.append(
            jnp.concatenate(
                [joined[at : at + 16, half : half + 128], joined[at + 16 : at + 32, half : half + 128]],
                axis=1,
            )
        )
    ordered = mm(
        one_hot(512, 512, lambda r: (r & 31) * 16 + (r >> 5)), jnp.concatenate(blocks, axis=0)
    ).astype(BF)
    dec_ref[0:512] = ordered[:, 0:128]
    dec_ref[512:1024] = ordered[:, 128:256]

    remote(got1, got1, s1_send, s1_recv, partner).wait_recv()
    total = pair[pl.ds(pl.multiple_of(xy * PIECE, 16), PIECE), :].astype(F32)
    for k in range(15):
        total = total + got1[k].astype(F32)
    got2[chip_z] = total.astype(BF)

    here = got2.at[chip_z]
    for step in Z_STEPS:
        remote(here, here, s2_send, s2_recv, z_peer(step)).start()

    seven = got2.at[0:7]
    remote(seven, seven, s2_send, s2_recv, partner).wait_recv()

    total = got2[0].astype(F32)
    for k in range(1, 8):
        total = total + got2[k].astype(F32)
    spot = pl.multiple_of(mine + xy * PIECE, 16)
    full[pl.ds(spot, PIECE), :] = total.astype(BF)

    def pass_on(q):
        here = full.at[pl.ds(pl.multiple_of(mine + q * PIECE, 16), PIECE)]
        remote(here, here, s4_send, s4_recv, partner).start()

    here = full.at[pl.ds(spot, PIECE)]
    for index, step in enumerate(XY_STEPS):
        remote(here, here, s3_send, s3_recv.at[index], xy_peer(step)[1]).start()
    pass_on(xy)

    halo_arrived(*g_halo)
    for zi in range(6):
        for yi in range(6):
            if zi in (0, 5) or yi in (0, 5):
                spread_grad(gh[zi, yi], zi * 6 + yi)
    back_up = uwt[...].reshape(2048, 64)
    flat = []
    for iz in range(2):
        columns = []
        for iy in range(2):
            columns.append(
                jnp.concatenate(
                    [
                        hgx[(2 * iz + kz) * 6 + 2 * iy + ky]
                        for kz in range(4)
                        for ky in range(4)
                    ],
                    axis=0,
                )
            )
        both = mm_tn(back_up, jnp.concatenate(columns, axis=1)).astype(BF)
        flat += [both[:, 0:128], both[:, 128:256]]
    order = one_hot(256, 256, lambda r: (r & 3) * 64 + (r >> 2))
    fgrad_ref[...] = mm(order, jnp.concatenate(flat, axis=0)).astype(BF)

    for index in reversed(range(15)):
        dx, dy = XY_STEPS[index]
        remote(here, here, s3_send, s3_recv.at[index], partner).wait_recv()
        pass_on(xy_peer((-dx, -dy))[0])

    halo_sent(*f_halo)
    halo_sent(*c_halo)
    halo_sent(*g_halo)
    remote(got1, got1, s1_send, s1_recv, partner).wait_send()
    remote(seven, seven, s2_send, s2_recv, partner).wait_send()
    remote(got1, got1, s3_send, s1_recv, partner).wait_send()
    def convert(half):
        start = pl.multiple_of(half * HALF, 16)
        scale = 1.0 / math.sqrt(131072)
        for unit in range(16):
            sy, vz, kx = unit // 8, unit // 4 % 2, unit % 4
            rows = full[pl.ds(start + unit * 32, 32), :].astype(F32) * scale
            for vy in range(2):
                k = half * 16 + vz * 32 + (2 * vy + sy) * 4 + kx
                ugrad_ref[pl.ds(k, 32, stride=64), :] = rows[:, vy * 64 : vy * 64 + 64]
        scale = 1.0 / math.sqrt(1048576)
        for unit in range(5):
            rows = full[pl.ds(start + 512 + unit * 32, 32), :].astype(F32) * scale
            for dx in range(3):
                at = pl.multiple_of(half * 384 + (unit * 3 + dx) * 32, 8)
                cgrad_ref[pl.ds(at, 32), :] = rows[:, dx * 32 : dx * 32 + 32]

    convert(core)
    here = full.at[pl.ds(mine, HALF)]
    remote(here, here, s4_send, s4_recv, partner).wait()

    convert(1 - core)


def write_out(*refs):
    sources, targets, sem = refs[0:4], refs[4:8], refs[8]
    copies = [pltpu.make_async_copy(sources[k], targets[k], sem.at[k]) for k in range(4)]
    for copy in copies:
        copy.start()
    for copy in copies:
        copy.wait()


def in_hbm(x):
    return pltpu.with_memory_space_constraint(x, pltpu.HBM)


def shards(features, up_weight, conv_weight, out_grad, labels):
    dma = pltpu.SemaphoreType.DMA
    vmem = pltpu.VMEM
    shapes = (
        jax.ShapeDtypeStruct((1024, 128), BF),
        jax.ShapeDtypeStruct((256, 128), BF),
        jax.ShapeDtypeStruct((2048, 64), F32),
        jax.ShapeDtypeStruct((864, 32), F32),
    )
    results = pl.pallas_call(
        kernel,
        out_shape=tuple(vmem(shape.shape, shape.dtype) for shape in shapes),
        in_specs=[pl.BlockSpec(memory_space=pl.ANY)] * 5,
        out_specs=[pl.BlockSpec(memory_space=vmem)] * 4,
        scratch_shapes=[
            vmem((256, 128), BF),
            vmem((2048, 64), BF),
            vmem((864, 32), BF),
            vmem((1024, 128), BF),
            vmem((32, 128), jnp.int32),
            dma((5,)),
            vmem((4, 4, 64, 128), BF),
            vmem((6, 6, 32, 256), BF),
            vmem((6, 6, 32, 256), BF),
            vmem((16, 192, 128), BF),
            vmem((3456, 256), BF),
            vmem((3456, 256), BF),
            vmem((36, 128, 128), BF),
            vmem((6, 6, 32, 256), BF),
            vmem((2048, 64), F32),
            vmem((64, 32, 64), BF),
            vmem((256, 768), BF),
            vmem((128, 1728), BF),
            vmem((128, 1728), BF),
            vmem((512, 256), BF),
            vmem((2 * HALF, 128), BF),
            vmem((HALF, 128), BF),
            vmem((HALF, 128), BF),
            vmem((15, PIECE, 128), BF),
            vmem((8, PIECE, 128), BF),
            vmem((2 * HALF, 128), BF),
            dma((8,)), dma((8,)), dma((8,)), dma((8,)), dma((8,)), dma((8,)),
            dma((2,)), dma((2,)), dma, dma, dma, dma, dma, dma((16,)), dma, dma,
        ],
        compiler_params=pltpu.CompilerParams(
            collective_id=0, has_side_effects=True, vmem_limit_bytes=40 * 1024 * 1024
        ),
        name="decoder_step",
    )(
        in_hbm(features.reshape(256, 128)),
        in_hbm(jnp.transpose(up_weight, (1, 2, 3, 4, 0)).reshape(2048, 64)),
        in_hbm(jnp.transpose(conv_weight, (2, 3, 4, 0, 1)).reshape(864, 32)),
        in_hbm(jnp.transpose(out_grad.reshape(32, 4, 4, 2, 128), (0, 1, 3, 2, 4)).reshape(1024, 128)),
        in_hbm(jnp.transpose(labels.reshape(4, 4, 2, 128), (0, 2, 1, 3)).reshape(32, 128)),
    )
    decoded, features_grad, up_grad, conv_grad = pl.pallas_call(
        write_out,
        out_shape=shapes,
        in_specs=[pl.BlockSpec(memory_space=pl.ANY)] * 4,
        out_specs=[pl.BlockSpec(memory_space=pl.ANY)] * 4,
        scratch_shapes=[dma((4,))],
        compiler_params=pltpu.CompilerParams(vmem_limit_bytes=40 * 1024 * 1024),
        name="write_out",
    )(*results)
    return (
        jnp.transpose(decoded.reshape(32, 4, 2, 4, 128), (0, 1, 3, 2, 4)).reshape(32, 4, 4, 256),
        features_grad.reshape(64, 2, 2, 128),
        jnp.transpose(up_grad.reshape(32, 4, 4, 4, 64), (4, 0, 1, 2, 3)),
        jnp.transpose(conv_grad.reshape(3, 3, 3, 32, 32), (3, 4, 0, 1, 2)),
    )


def solution(mesh):
    in_specs = (P(None, "gz", "gy", None), P(), P(), P(None, "gz", "gy", None), P("gz", "gy", None))
    out_specs = (P(None, "gz", "gy", None), P(None, "gz", "gy", None), P(), P())
    return jax.shard_map(shards, mesh=mesh, in_specs=in_specs, out_specs=out_specs, check_vma=False)
```

```python
import math

import jax
import jax.numpy as jnp
from jax import lax
from jax.experimental import pallas as pl
from jax.experimental.pallas import tpu as pltpu
from jax.sharding import PartitionSpec as P

BF = jnp.bfloat16
F32 = jnp.float32
MESH = pl.DeviceIdType.MESH

NZ, NY = 8, 32
DIRECTIONS = [(0, 1), (0, -1), (1, 1), (-1, 1), (1, -1), (-1, -1), (1, 0), (-1, 0)]
XY_STEPS = sorted(
    [(dx, dy) for dx in range(4) for dy in range(4) if (dx, dy) != (0, 0)],
    key=lambda step: -(min(step[0], 4 - step[0]) + min(step[1], 4 - step[1])),
)
Z_STEPS = (4, 3, 5, 2, 6, 1, 7)
PIECE = 48
HALF = 16 * PIECE


def mm(a, b):
    return lax.dot_general(a, b, (((1,), (0,)), ((), ())), preferred_element_type=F32)


def mm_nt(a, b):
    return lax.dot_general(a, b, (((1,), (1,)), ((), ())), preferred_element_type=F32)


def mm_tn(a, b):
    return lax.dot_general(a, b, (((0,), (0,)), ((), ())), preferred_element_type=F32)


def one_hot(rows, cols, place):
    row = lax.broadcasted_iota(jnp.int32, (rows, cols), 0)
    col = lax.broadcasted_iota(jnp.int32, (rows, cols), 1)
    return jnp.where(place(row) == col, 1.0, 0.0).astype(BF)


def lane_masks(rows):
    lane = lax.broadcasted_iota(jnp.int32, (rows, 128), 1)
    return lane == 0, lane == 127


def before_lane(x, first):
    return jnp.where(first, 0.0, pltpu.roll(x, 1, 1))


def after_lane(x, last):
    return jnp.where(last, 0.0, pltpu.roll(x, 127, 1))


def halo_source(step, extent):
    if step == 0:
        return pl.ds(1, extent)
    return pl.ds(extent, 1) if step == 1 else pl.ds(1, 1)


def halo_target(step, extent):
    if step == 0:
        return pl.ds(1, extent)
    return pl.ds(0, 1) if step == 1 else pl.ds(extent + 1, 1)


def kernel(
    feat_hbm, up_hbm, conv_hbm, og_hbm, lab_hbm,
    dec_ref, fgrad_ref, ugrad_ref, cgrad_ref,
    feat_ref, up_ref, conv_ref, og_ref, lab_ref, load_sem,
    fh, ch, gh, fx, hx, cx, hgx, he,
    upf, uwt, t_up, t_fwd, t_bwd, dec,
    part, got0, pair, got1, got2, full,
    f_send, f_recv, c_send, c_recv, g_send, g_recv,
    s0_send, s0_recv, s1_send, s1_recv, s2_send, s2_recv, s3_send, s3_recv, s4_send, s4_recv,
):
    gz = lax.axis_index("gz")
    gy = lax.axis_index("gy")
    core = gz % 2
    z_lo = gz // 2
    z_hi = gy // 16
    xy = gy % 16
    chip_z = z_hi * 4 + z_lo
    partner = (gz + 1 - 2 * core, gy)

    def xy_peer(step):
        q = (xy // 4 + step[0]) % 4 * 4 + (xy % 4 + step[1]) % 4
        return q, (gz, z_hi * 16 + q)

    def z_peer(step):
        q = (chip_z + step) % 8
        return (q % 4) * 2 + core, (q // 4) * 16 + xy

    def exists(dz, dy):
        return (gz + dz >= 0) & (gz + dz < NZ) & (gy + dy >= 0) & (gy + dy < NY)

    barrier = pltpu.get_barrier_semaphore()
    for dz, dy in DIRECTIONS:
        @pl.when(exists(dz, dy))
        def _():
            pl.semaphore_signal(barrier, 1, device_id=(gz + dz, gy + dy), device_id_type=MESH)

    loads = [
        pltpu.make_async_copy(source, target, load_sem.at[index])
        for index, (source, target) in enumerate(
            (
                (feat_hbm, feat_ref),
                (og_hbm, og_ref),
                (lab_hbm, lab_ref),
                (up_hbm, up_ref),
                (conv_hbm, conv_ref),
            )
        )
    ]
    for load in loads:
        load.start()
    pl.semaphore_signal(barrier, 1, device_id=partner, device_id_type=MESH)

    for step in XY_STEPS:
        q, device = xy_peer(step)
        pl.semaphore_signal(barrier, 1, device_id=device, device_id_type=MESH)
        pl.semaphore_signal(
            barrier, 1, device_id=(partner[0], z_hi * 16 + q), device_id_type=MESH
        )
    for step in Z_STEPS:
        pl.semaphore_signal(barrier, 1, device_id=z_peer(step), device_id_type=MESH)

    loads[0].wait()
    local = mm(one_hot(256, 256, lambda r: (r & 63) * 4 + (r >> 6)), feat_ref[...]).astype(BF)
    for k in range(4):
        fh[1 + k // 2, 1 + k % 2] = local[k * 64 : (k + 1) * 64]

    split = one_hot(256, 256, lambda r: (r & 1) * 128 + (r >> 1))
    loads[1].wait()
    loads[2].wait()
    masked = (og_ref[...].reshape(32, 32, 128) * lab_ref[...].astype(BF)[None]).reshape(1024, 128)
    rows = mm(
        one_hot(512, 512, lambda r: (r & 15) * 32 + (r >> 4)),
        jnp.concatenate([masked[0:512], masked[512:1024]], axis=1),
    ).astype(BF)
    for k in range(16):
        for half in range(2):
            at = ((k // 4) * 8 + half * 4 + k % 4) * 16
            for group in range(2):
                dec[k * 32 + group * 16 : k * 32 + group * 16 + 16, half * 128 : half * 128 + 128] = (
                    rows[at : at + 16, group * 128 : group * 128 + 128]
                )
    local = mm(dec[...], split).astype(BF)
    for k in range(16):
        ch[1 + k // 4, 1 + k % 4] = local[k * 32 : (k + 1) * 32]

    beside = 1 * (gz > 0) + 1 + 1 * (gz < NZ - 1)
    beside = beside * (1 * (gy > 0) + 1 + 1 * (gy < NY - 1)) - 1
    pl.semaphore_wait(barrier, beside + 1 + 30 + 7)

    def halo_copy(buf, extent, index, send, recv):
        dz, dy = DIRECTIONS[index]
        return pltpu.make_async_remote_copy(
            src_ref=buf.at[halo_source(dz, extent), halo_source(dy, extent)],
            dst_ref=buf.at[halo_target(dz, extent), halo_target(dy, extent)],
            send_sem=send.at[index],
            recv_sem=recv.at[index],
            device_id=(gz + dz, gy + dy),
            device_id_type=MESH,
        )

    def halo_start(side, *halos):
        for what in halos:
            for index, (dz, dy) in sorted(enumerate(DIRECTIONS), key=lambda item: abs(item[1][0])):
                if dy == side:
                    @pl.when(exists(dz, dy))
                    def _():
                        halo_copy(what[0], what[1], index, what[2], what[3]).start()

    def halo_start_all(*halos):
        @pl.when(gy % 16 == 0)
        def _():
            halo_start(-1, *halos)

        halo_start(1, *halos)
        halo_start(0, *halos)

        @pl.when(gy % 16 > 0)
        def _():
            halo_start(-1, *halos)

    def halo_arrived(*what):
        for index, (dz, dy) in enumerate(DIRECTIONS):
            @pl.when(exists(-dz, -dy))
            def _():
                halo_copy(what[0], what[1], index, what[2], what[3]).wait_recv()

    def halo_sent(*what):
        for index, (dz, dy) in enumerate(DIRECTIONS):
            @pl.when(exists(dz, dy))
            def _():
                halo_copy(what[0], what[1], index, what[2], what[3]).wait_send()

    f_halo = (fh, 2, f_send, f_recv)
    c_halo = (ch, 4, c_send, c_recv)
    g_halo = (gh, 4, g_send, g_recv)
    halo_start_all(f_halo, c_halo)

    @pl.when(gz == 0)
    def _():
        for buf in (fh, ch, gh):
            buf[0] = jnp.zeros(buf.shape[1:], BF)

    @pl.when(gz == NZ - 1)
    def _():
        for buf in (fh, ch, gh):
            buf[buf.shape[0] - 1] = jnp.zeros(buf.shape[1:], BF)

    @pl.when(gy == 0)
    def _():
        for buf in (fh, ch, gh):
            for k in range(buf.shape[0]):
                buf[k, 0] = jnp.zeros(buf.shape[2:], BF)

    @pl.when(gy == NY - 1)
    def _():
        for buf in (fh, ch, gh):
            for k in range(buf.shape[0]):
                buf[k, buf.shape[1] - 1] = jnp.zeros(buf.shape[2:], BF)

    loads[3].wait()
    loads[4].wait()
    upf[...] = up_ref[...].astype(F32)

    @pl.loop(0, 64)
    def _(k):
        uwt[k] = upf[pl.ds(k, 32, stride=64), :].astype(BF)

    for sz in range(2):
        for sy in range(2):
            for px in range(2):
                blocks = []
                for uz in range(2):
                    for uy in range(2):
                        base = (2 * (1 - uz) + sz) * 16 + (2 * (1 - uy) + sy) * 4
                        none = jnp.zeros((32, 64), BF)
                        if px == 0:
                            blocks += [uwt[base + 3], uwt[base + 1], none]
                        else:
                            blocks += [none, uwt[base + 2], uwt[base]]
                at = ((sz * 2 + sy) * 2 + px) * 32
                t_up[at : at + 32, :] = jnp.concatenate(blocks, axis=1)
    zero = jnp.zeros((32, 96), BF)
    taps = {}
    back = {}
    for dz in range(3):
        for dy in range(3):
            at = (dz * 3 + dy) * 96
            taps[dz, dy] = jnp.concatenate(
                [conv_ref[at + 32 * dx : at + 32 * dx + 32, :] for dx in range(3)], axis=1
            )
            back[2 - dz, 2 - dy] = conv_ref[at : at + 96, :].T
    for yo in range(4):
        for matrix, source in ((t_fwd, taps), (t_bwd, back)):
            matrix[yo * 32 : yo * 32 + 32, :] = jnp.concatenate(
                [
                    source[dz, yi - yo] if 0 <= yi - yo < 3 else zero
                    for dz in range(3)
                    for yi in range(6)
                ],
                axis=1,
            )

    first64, last64 = lane_masks(64)
    first, last = lane_masks(32)

    def spread_cotangent(zi, yi):
        row = ch[zi, yi]
        even, odd = row[:, 0:128], row[:, 128:256]
        at = (zi * 6 + yi) * 96
        cx[at : at + 32, 0:128] = odd
        cx[at : at + 32, 128:256] = after_lane(even.astype(F32), last).astype(BF)
        cx[at + 32 : at + 64, :] = row
        cx[at + 64 : at + 96, 0:128] = before_lane(odd.astype(F32), first).astype(BF)
        cx[at + 64 : at + 96, 128:256] = even

    for zi in range(1, 5):
        for yi in range(1, 5):
            spread_cotangent(zi, yi)

    halo_arrived(*f_halo)
    for k in range(16):
        row = fh[k // 4, k % 4]
        wide = row.astype(F32)
        fx[k, 0:64] = before_lane(wide, first64).astype(BF)
        fx[k, 64:128] = row
        fx[k, 128:192] = after_lane(wide, last64).astype(BF)

    for jz in range(3):
        columns = []
        for jy in range(3):
            columns.append(
                jnp.concatenate(
                    [fx[(jz + uz) * 4 + jy + uy] for uz in range(2) for uy in range(2)], axis=0
                )
            )
        lifted = jnp.maximum(mm(t_up[...], jnp.concatenate(columns, axis=1)), 0.0)
        for sz in range(2):
            for sy in range(2):
                for jy in range(3):
                    at = (sz * 2 + sy) * 64
                    even = lifted[at : at + 32, jy * 128 : jy * 128 + 128]
                    odd = lifted[at + 32 : at + 64, jy * 128 : jy * 128 + 128]
                    zo, yo = jz * 2 + sz, jy * 2 + sy
                    at = (zo * 6 + yo) * 96
                    even_b, odd_b = even.astype(BF), odd.astype(BF)
                    hx[pl.ds(at, 32), 0:128] = before_lane(odd, first).astype(BF)
                    hx[pl.ds(at, 32), 128:256] = even_b
                    hx[pl.ds(at + 32, 32), 0:128] = even_b
                    hx[pl.ds(at + 32, 32), 128:256] = odd_b
                    hx[pl.ds(at + 64, 32), 0:128] = odd_b
                    hx[pl.ds(at + 64, 32), 128:256] = after_lane(even, last).astype(BF)
                    he[zo, yo, :, 0:128] = even_b
                    he[zo, yo, :, 128:256] = odd_b

    @pl.when(gz == 0)
    def _():
        hx[0:576] = jnp.zeros((576, 256), BF)

    @pl.when(gz == NZ - 1)
    def _():
        hx[2880:3456] = jnp.zeros((576, 256), BF)

    @pl.when(gy == 0)
    def _():
        for zi in range(6):
            hx[zi * 576 : zi * 576 + 96] = jnp.zeros((96, 256), BF)

    @pl.when(gy == NY - 1)
    def _():
        for zi in range(6):
            hx[zi * 576 + 480 : zi * 576 + 576] = jnp.zeros((96, 256), BF)

    def remote(src, dst, send, recv, device):
        return pltpu.make_async_remote_copy(
            src_ref=src, dst_ref=dst, send_sem=send, recv_sem=recv,
            device_id=device, device_id_type=MESH,
        )

    mine = pl.multiple_of(core * HALF, 16)
    other = pl.multiple_of((1 - core) * HALF, 16)
    for half in range(2):
        part[half * HALF + 512 : (half + 1) * HALF] = jnp.zeros((HALF - 512, 128), BF)
    for dz in range(3):
        total = mm_nt(
            jnp.concatenate([hx[(zo + dz) * 576 : (zo + dz + 1) * 576, :] for zo in range(4)], axis=1),
            jnp.concatenate([ch[1 + zo, 1:5].reshape(128, 256) for zo in range(4)], axis=1),
        )
        for dy in range(3):
            grad = total[dy * 96 : dy * 96 + 96, 0:32]
            for yo in range(1, 4):
                grad = grad + total[(yo + dy) * 96 : (yo + dy) * 96 + 96, yo * 32 : yo * 32 + 32]
            grad = grad.T
            for half in range(2):
                if 0 <= dz * 3 + dy - 4 * half < 5:
                    at = half * HALF + 512 + (dz * 3 + dy - 4 * half) * 32
                    part[at : at + 32, 0:96] = grad.astype(BF)

    copy_conv = remote(
        part.at[pl.ds(pl.multiple_of(other + 512, 16), 256)], got0.at[512:768],
        s0_send.at[0], s0_recv.at[0], partner,
    )
    copy_conv.start()

    halo_arrived(*c_halo)
    for zi in range(6):
        for yi in range(6):
            if zi in (0, 5) or yi in (0, 5):
                spread_cotangent(zi, yi)

    for zo in range(4):
        before = mm(t_bwd[...], cx[pl.ds(zo * 576, 1728), :])
        for yo in range(4):
            grad = jnp.where(
                he[1 + zo, 1 + yo].astype(F32) > 0.0, before[yo * 32 : yo * 32 + 32], 0.0
            )
            gh[1 + zo, 1 + yo] = grad.astype(BF)

    halo_start_all(g_halo)

    def spread_grad(row, slot):
        even, odd = row[:, 0:128], row[:, 128:256]
        hgx[slot, 0:32] = before_lane(odd.astype(F32), first).astype(BF)
        hgx[slot, 32:64] = even
        hgx[slot, 64:96] = odd
        hgx[slot, 96:128] = after_lane(even.astype(F32), last).astype(BF)

    for zi in range(1, 5):
        for yi in range(1, 5):
            spread_grad(gh[zi, yi], zi * 6 + yi)

    def up_terms(sz):
        for sy in range(2):
            lhs, rhs = [], []
            for turn in range(2):
                jz = turn + 1 - sz
                for jy in (0, 1) if sy else (1, 2):
                    lhs.append(hgx[(2 * jz + sz) * 6 + 2 * jy + sy])
                    rhs.append(
                        jnp.concatenate(
                            [fh[jz + 1 - vz, jy + 1 - vy] for vz in range(2) for vy in range(2)],
                            axis=0,
                        )
                    )
            grad = mm_nt(jnp.concatenate(lhs, axis=1), jnp.concatenate(rhs, axis=1)).astype(BF)
            at = pl.multiple_of(sz * HALF + sy * 256, 16)
            part[pl.ds(at, 128), :] = grad[:, 0:128]
            part[pl.ds(at + 128, 128), :] = grad[:, 128:256]

    up_terms(1 - core)
    copy_up = remote(
        part.at[pl.ds(other, 512)], got0.at[0:512], s0_send.at[1], s0_recv.at[1], partner
    )
    copy_up.start()
    up_terms(core)
    copy_conv.wait()
    copy_up.wait()
    pair[...] = (part[pl.ds(mine, HALF), :].astype(F32) + got0[...].astype(F32)).astype(BF)

    for index, step in enumerate(XY_STEPS):
        q, device = xy_peer(step)
        remote(
            pair.at[pl.ds(pl.multiple_of(q * PIECE, 16), PIECE)], got1.at[index],
            s1_send, s1_recv, device,
        ).start()

    for zo in range(4):
        done = mm(t_fwd[...], hx[pl.ds(zo * 576, 1728), :])
        dec[pl.ds(zo * 128, 128), :] = done.astype(BF)

    joined = mm_nt(dec[...], split).astype(BF)
    blocks = []
    for k in range(32):
        at = ((k // 8) * 4 + k % 4) * 32
        half = (k // 4) % 2 * 128
        blocks.append(
            jnp.concatenate(
                [joined[at : at + 16, half : half + 128], joined[at + 16 : at + 32, half : half + 128]],
                axis=1,
            )
        )
    ordered = mm(
        one_hot(512, 512, lambda r: (r & 31) * 16 + (r >> 5)), jnp.concatenate(blocks, axis=0)
    ).astype(BF)
    dec_ref[0:512] = ordered[:, 0:128]
    dec_ref[512:1024] = ordered[:, 128:256]

    remote(got1, got1, s1_send, s1_recv, partner).wait_recv()
    total = pair[pl.ds(pl.multiple_of(xy * PIECE, 16), PIECE), :].astype(F32)
    for k in range(15):
        total = total + got1[k].astype(F32)
    got2[chip_z] = total.astype(BF)

    here = got2.at[chip_z]
    for step in Z_STEPS:
        remote(here, here, s2_send, s2_recv, z_peer(step)).start()

    seven = got2.at[0:7]
    remote(seven, seven, s2_send, s2_recv, partner).wait_recv()

    total = got2[0].astype(F32)
    for k in range(1, 8):
        total = total + got2[k].astype(F32)
    spot = pl.multiple_of(mine + xy * PIECE, 16)
    full[pl.ds(spot, PIECE), :] = total.astype(BF)

    here = full.at[pl.ds(spot, PIECE)]
    for index, step in enumerate(XY_STEPS):
        q, device = xy_peer(step)
        remote(here, here, s3_send, s3_recv.at[index], device).start()
        remote(here, here, s4_send, s4_recv, (partner[0], z_hi * 16 + q)).start()
    remote(here, here, s4_send, s4_recv, partner).start()

    halo_arrived(*g_halo)
    for zi in range(6):
        for yi in range(6):
            if zi in (0, 5) or yi in (0, 5):
                spread_grad(gh[zi, yi], zi * 6 + yi)
    back_up = uwt[...].reshape(2048, 64)
    flat = []
    for iz in range(2):
        columns = []
        for iy in range(2):
            columns.append(
                jnp.concatenate(
                    [
                        hgx[(2 * iz + kz) * 6 + 2 * iy + ky]
                        for kz in range(4)
                        for ky in range(4)
                    ],
                    axis=0,
                )
            )
        both = mm_tn(back_up, jnp.concatenate(columns, axis=1)).astype(BF)
        flat += [both[:, 0:128], both[:, 128:256]]
    order = one_hot(256, 256, lambda r: (r & 3) * 64 + (r >> 2))
    fgrad_ref[...] = mm(order, jnp.concatenate(flat, axis=0)).astype(BF)

    for index in reversed(range(15)):
        remote(here, here, s3_send, s3_recv.at[index], partner).wait_recv()

    halo_sent(*f_halo)
    halo_sent(*c_halo)
    halo_sent(*g_halo)
    remote(got1, got1, s1_send, s1_recv, partner).wait_send()
    remote(seven, seven, s2_send, s2_recv, partner).wait_send()
    remote(got1, got1, s3_send, s1_recv, partner).wait_send()
    def convert(half):
        start = pl.multiple_of(half * HALF, 16)
        scale = 1.0 / math.sqrt(131072)
        for unit in range(16):
            sy, vz, kx = unit // 8, unit // 4 % 2, unit % 4
            rows = full[pl.ds(start + unit * 32, 32), :].astype(F32) * scale
            for vy in range(2):
                k = half * 16 + vz * 32 + (2 * vy + sy) * 4 + kx
                ugrad_ref[pl.ds(k, 32, stride=64), :] = rows[:, vy * 64 : vy * 64 + 64]
        scale = 1.0 / math.sqrt(1048576)
        for unit in range(5):
            rows = full[pl.ds(start + 512 + unit * 32, 32), :].astype(F32) * scale
            for dx in range(3):
                at = pl.multiple_of(half * 384 + (unit * 3 + dx) * 32, 8)
                cgrad_ref[pl.ds(at, 32), :] = rows[:, dx * 32 : dx * 32 + 32]

    convert(core)
    here = full.at[pl.ds(mine, HALF)]
    remote(here, here, s4_send, s4_recv, partner).wait()

    convert(1 - core)


def write_out(*refs):
    sources, targets, sem = refs[0:4], refs[4:8], refs[8]
    copies = [pltpu.make_async_copy(sources[k], targets[k], sem.at[k]) for k in range(4)]
    for copy in copies:
        copy.start()
    for copy in copies:
        copy.wait()


def in_hbm(x):
    return pltpu.with_memory_space_constraint(x, pltpu.HBM)


def shards(features, up_weight, conv_weight, out_grad, labels):
    dma = pltpu.SemaphoreType.DMA
    vmem = pltpu.VMEM
    shapes = (
        jax.ShapeDtypeStruct((1024, 128), BF),
        jax.ShapeDtypeStruct((256, 128), BF),
        jax.ShapeDtypeStruct((2048, 64), F32),
        jax.ShapeDtypeStruct((864, 32), F32),
    )
    results = pl.pallas_call(
        kernel,
        out_shape=tuple(vmem(shape.shape, shape.dtype) for shape in shapes),
        in_specs=[pl.BlockSpec(memory_space=pl.ANY)] * 5,
        out_specs=[pl.BlockSpec(memory_space=vmem)] * 4,
        scratch_shapes=[
            vmem((256, 128), BF),
            vmem((2048, 64), BF),
            vmem((864, 32), BF),
            vmem((1024, 128), BF),
            vmem((32, 128), jnp.int32),
            dma((5,)),
            vmem((4, 4, 64, 128), BF),
            vmem((6, 6, 32, 256), BF),
            vmem((6, 6, 32, 256), BF),
            vmem((16, 192, 128), BF),
            vmem((3456, 256), BF),
            vmem((3456, 256), BF),
            vmem((36, 128, 128), BF),
            vmem((6, 6, 32, 256), BF),
            vmem((2048, 64), F32),
            vmem((64, 32, 64), BF),
            vmem((256, 768), BF),
            vmem((128, 1728), BF),
            vmem((128, 1728), BF),
            vmem((512, 256), BF),
            vmem((2 * HALF, 128), BF),
            vmem((HALF, 128), BF),
            vmem((HALF, 128), BF),
            vmem((15, PIECE, 128), BF),
            vmem((8, PIECE, 128), BF),
            vmem((2 * HALF, 128), BF),
            dma((8,)), dma((8,)), dma((8,)), dma((8,)), dma((8,)), dma((8,)),
            dma((2,)), dma((2,)), dma, dma, dma, dma, dma, dma((16,)), dma, dma,
        ],
        compiler_params=pltpu.CompilerParams(
            collective_id=0, has_side_effects=True, vmem_limit_bytes=40 * 1024 * 1024
        ),
        name="decoder_step",
    )(
        in_hbm(features.reshape(256, 128)),
        in_hbm(jnp.transpose(up_weight, (1, 2, 3, 4, 0)).reshape(2048, 64)),
        in_hbm(jnp.transpose(conv_weight, (2, 3, 4, 0, 1)).reshape(864, 32)),
        in_hbm(jnp.transpose(out_grad.reshape(32, 4, 4, 2, 128), (0, 1, 3, 2, 4)).reshape(1024, 128)),
        in_hbm(jnp.transpose(labels.reshape(4, 4, 2, 128), (0, 2, 1, 3)).reshape(32, 128)),
    )
    decoded, features_grad, up_grad, conv_grad = pl.pallas_call(
        write_out,
        out_shape=shapes,
        in_specs=[pl.BlockSpec(memory_space=pl.ANY)] * 4,
        out_specs=[pl.BlockSpec(memory_space=pl.ANY)] * 4,
        scratch_shapes=[dma((4,))],
        compiler_params=pltpu.CompilerParams(vmem_limit_bytes=40 * 1024 * 1024),
        name="write_out",
    )(*results)
    return (
        jnp.transpose(decoded.reshape(32, 4, 2, 4, 128), (0, 1, 3, 2, 4)).reshape(32, 4, 4, 256),
        features_grad.reshape(64, 2, 2, 128),
        jnp.transpose(up_grad.reshape(32, 4, 4, 4, 64), (4, 0, 1, 2, 3)),
        jnp.transpose(conv_grad.reshape(3, 3, 3, 32, 32), (3, 4, 0, 1, 2)),
    )


def solution(mesh):
    in_specs = (P(None, "gz", "gy", None), P(), P(), P(None, "gz", "gy", None), P("gz", "gy", None))
    out_specs = (P(None, "gz", "gy", None), P(None, "gz", "gy", None), P(), P())
    return jax.shard_map(shards, mesh=mesh, in_specs=in_specs, out_specs=out_specs, check_vma=False)
```
